512 devices in a mesh: section: 16 (over z_lo, y), dp: 32 (over z_hi, x, core).
Axes of the slice: x: 4, y: 4, z: 16 (z_hi: 4, z_lo: 4; z = z_hi * 4 + z_lo), core: 2. Of those that a mesh axis runs over, the one named last changes fastest.
Arguments:
- acts: bfloat16 [2, 16, 2048, 4096], P(None, 'section', 'dp')
- norm_gain: float32 [16, 4096], P('section'), may hold values from 0.5 to 1.5
- value_grads: bfloat16 [2, 16, 2048, 512], P(None, 'section', 'dp')
- master: float32 [16, 4096, 512], P('section', 'dp'), may hold values from -0.09375 to 0.09375
- moment1: float32 [16, 4096, 512], P('section', 'dp'), may hold values from -6 to 6
- moment2: float32 [16, 4096, 512], P('section', 'dp'), may hold values from 0.25 to 4
- next_acts: bfloat16 [2, 16, 2048, 4096], P(None, 'section', 'dp')
- reward_table: bfloat16 [5, 4096], replicated, may hold values from -6 to 6
- reward_ids: int32 [2, 32], replicated, may hold values from 0 to 4
Outputs:
- input_grads: bfloat16 [2, 16, 2048, 4096], P(None, 'section', 'dp')
- moment1_new: float32 [16, 4096, 512], P('section', 'dp')
- moment2_new: float32 [16, 4096, 512], P('section', 'dp')
- fresh_values: bfloat16 [2, 16, 2048, 512], P(None, 'section', 'dp')
The draws below stay inside these ranges and needn't reach their ends.
All inputs are finite; a program needn't handle non-finite values.
Results may differ from the reference program's by a relative error of at most 0.015.
Values may be sent and summed in bfloat16 or wider, within the bound.
No kernel may reach another device: no remote copies, remote signals or barrier semaphores. Data moves between devices by JAX's collectives and lax.ppermute only.
A program may use at most 64 MiB of HBM per device.

```python
import math
import jax
import jax.numpy as jnp
from jax import lax

D = 4096
KVW = 512
TOK_DEV = 64
MB = 2
BINS = 5
SECTIONS = 16
TOKENS = 2048
SEQS = 32
N_DP = 32


def rough_field(key, shape, spread):
    keys = jax.random.split(key, 3)
    base = jax.random.normal(keys[0], shape, jnp.float32)
    rows = jnp.exp(jax.random.uniform(keys[1], shape[:-1] + (1,), jnp.float32, -spread, spread))
    cols = jnp.exp(jax.random.uniform(keys[2], (1,) * (len(shape) - 1) + (shape[-1],), jnp.float32, -spread, spread))
    return base * rows * cols


def draw_acts(key, part):
    key = jax.random.fold_in(key, 11)
    return rough_field(key, (MB, SECTIONS, TOKENS, D), 1.15).astype(jnp.bfloat16)


def draw_next_acts(key, part):
    key = jax.random.fold_in(key, 23)
    return rough_field(key, (MB, SECTIONS, TOKENS, D), 1.15).astype(jnp.bfloat16)


def draw_value_grads(key, part):
    key = jax.random.fold_in(key, 37)
    shape = (MB, SECTIONS, TOKENS, KVW)
    layer = jax.lax.broadcasted_iota(jnp.float32, (1, SECTIONS, 1, 1), 1)
    ramp = 1.0 + 2.0 * layer / max(SECTIONS - 1, 1)
    field = rough_field(key, shape, 1.15)
    return (field * ramp).astype(jnp.bfloat16)


def touch_ends(array, stream_key, low, top_value):
    dims = array.shape
    index_at = [jax.random.randint(jax.random.fold_in(stream_key, axis), (), 0, dims[axis]) for axis in range(len(dims))]
    array = array.at[tuple(index_at)].set(low)
    longest = dims.index(max(dims))
    index_at[longest] = (index_at[longest] + 1) % dims[longest]
    return array.at[tuple(index_at)].set(top_value)


def shard_levels(own_key, dims, cuts, low, top_value):
    loudness, own = 1.0, jax.random.fold_in(own_key, 6)
    for position, shards_of in cuts:
        heights = jnp.exp(jax.random.uniform(jax.random.fold_in(own, position), (shards_of,), jnp.float32, low / len(cuts), top_value / len(cuts)))
        loudness = loudness * jnp.repeat(heights, dims[position] // shards_of).reshape([-1 if axis == position else 1 for axis in range(len(dims))])
    return loudness


def centred(rng, extent, deviation, most, cuts=(), kind=jnp.bfloat16):
    values = jax.random.normal(rng, extent, jnp.float32) * deviation
    if len(cuts) > 0:
        values = shard_levels(rng, extent, cuts, -0.22, 0.18) * values
    return jnp.clip(values, min=-most, max=most).astype(kind)


def setup_inputs(seed: int = 0) -> dict:
    seeds = jax.random.split(jax.random.key(seed), 10)
    return {
        "acts": draw_acts(jax.random.fold_in(seeds[9], 71), 0),
        "norm_gain": jnp.clip(1.0 + 0.1 * jax.random.normal(seeds[1], (SECTIONS, D), jnp.float32), 0.5, 1.5),
        "value_grads": draw_value_grads(jax.random.fold_in(seeds[9], 71), 0),
        "master": centred(seeds[3], (SECTIONS, D, KVW), D ** -0.5, 0.09375, ((0, 16), (1, 32)), jnp.float32),
        "moment1": centred(seeds[4], (SECTIONS, D, KVW), 1.0, 6.0, ((0, 16), (1, 32)), jnp.float32),
        "moment2": jnp.clip(jnp.exp(math.log(4.0) - 2.7725887 * jax.random.uniform(seeds[5], (SECTIONS, D, KVW), jnp.float32) ** shard_levels(seeds[5], (SECTIONS, D, KVW), ((0, 16), (1, 32)), -0.2, 0.2)), 0.25, 4.0),
        "next_acts": draw_next_acts(jax.random.fold_in(seeds[9], 71), 0),
        "reward_table": centred(seeds[7], (BINS, D), 1.0, 6.0),
        "reward_ids": touch_ends(jax.random.randint(seeds[8], (MB, SEQS), 0, BINS), jax.random.fold_in(seeds[8], 1), 0, BINS - 1).astype(jnp.int32),
    }


rms_epsilon = 1e-05
clip_level = 1.0
beta_first = 0.9
beta_second = 0.95
learn_rate = 0.001
decay_rate = 0.01
adam_epsilon = 1e-08
bias_first = 1.0 - 0.9 ** 10
bias_second = 1.0 - 0.95 ** 10

def normalize(floats):
    inverse = lax.rsqrt(lax.optimization_barrier(jnp.mean(floats * floats, axis=-1, keepdims=True)) + rms_epsilon)
    return (floats * inverse, inverse)

def reference(acts, norm_gain, value_grads, master, moment1, moment2, next_acts, reward_table, reward_ids):
    weights_old = master.astype(jnp.bfloat16)

    def layer_back(running, items):
        inputs, gain, values, weight = items
        scaled, inverse = normalize(inputs.astype(jnp.float32))
        normed = (scaled * gain).astype(jnp.bfloat16)
        upstream = jnp.einsum('mtk,dk->mtd', values.astype(jnp.float32), weight.astype(jnp.float32))
        mixed = gain * upstream
        branch = inverse * (mixed - scaled * lax.optimization_barrier(jnp.mean(scaled * mixed, axis=-1, keepdims=True)))
        running = running + branch
        blocks_h = normed.reshape(MB, N_DP, TOK_DEV, D).astype(jnp.float32)
        blocks_v = values.reshape(MB, N_DP, TOK_DEV, KVW).astype(jnp.float32)
        parts = jnp.einsum('mntd,mntk->ndk', blocks_h, blocks_v)
        rounded = lax.optimization_barrier(parts.astype(jnp.bfloat16)).astype(jnp.float32)
        return (running, (running.astype(jnp.bfloat16), lax.optimization_barrier(jnp.sum(rounded, axis=0))))
    items = (jnp.transpose(acts, (1, 0, 2, 3)), norm_gain, jnp.transpose(value_grads, (1, 0, 2, 3)), weights_old)
    start_sum = jnp.zeros((MB, TOKENS, D), jnp.float32)
    unused, (stacked, grad) = lax.scan(layer_back, start_sum, items, reverse=True)
    input_grads = jnp.transpose(stacked, (1, 0, 2, 3))
    rms = jnp.sqrt(jnp.sum(grad * grad) / (SECTIONS * D * KVW) + 1e-12)
    clip = jnp.minimum(1.0, clip_level / rms)
    clipped = grad * clip
    moment1_new = beta_first * moment1 + (1.0 - beta_first) * clipped
    moment2_new = beta_second * moment2 + (1.0 - beta_second) * clipped * clipped
    update = moment1_new / bias_first / (jnp.sqrt(moment2_new / bias_second) + adam_epsilon) + decay_rate * master
    weights_new = (master - learn_rate * update).astype(jnp.bfloat16)
    positions = jnp.arange(TOKENS, dtype=jnp.int32)
    starts = positions % TOK_DEV == 0
    seq_index = (positions // TOK_DEV).astype(jnp.int32)
    row_bins = reward_ids[:, seq_index]
    embeds = reward_table[row_bins]
    first_layer = jnp.where(starts[None, :, None], embeds, next_acts[:, 0])
    fresh_inputs = next_acts.at[:, 0].set(first_layer)

    def layer_forward(items_next):
        inputs, gain, weight = items_next
        scaled, inverse = normalize(inputs.astype(jnp.float32))
        fresh_normed = (scaled * gain).astype(jnp.bfloat16)
        result = jnp.einsum('mtd,dk->mtk', fresh_normed.astype(jnp.float32), weight.astype(jnp.float32))
        return result.astype(jnp.bfloat16)
    fresh = lax.map(layer_forward, (jnp.transpose(fresh_inputs, (1, 0, 2, 3)), norm_gain, weights_new))
    fresh_values = jnp.transpose(fresh, (1, 0, 2, 3))
    return (input_grads, moment1_new, moment2_new, fresh_values)
```

```python
import jax
import jax.numpy as jnp
from jax import lax
from jax.sharding import Mesh
from jax.sharding import PartitionSpec as P

rms_epsilon = 1e-05
clip_level = 1.0
beta_first = 0.9
beta_second = 0.95
learn_rate = 0.001
decay_rate = 0.01
adam_epsilon = 1e-08
bias_first = 1.0 - 0.9**10
bias_second = 1.0 - 0.95**10

factors = {"section": (4, 4), "dp": (4, 4, 2)}
axes = ("zlo", "y", "zhi", "x", "core")
section = ("zlo", "y")
dp = ("zhi", "x", "core")
near = ("x", "core")
f32 = jnp.float32
bf16 = jnp.bfloat16


def exchange(blocks, axis):
    return lax.all_to_all(blocks, axis, 0, 0)


def total(value, axis):
    size = lax.axis_size(axis)
    return jnp.sum(exchange(jnp.broadcast_to(value, (size,) + value.shape), axis), axis=0)


def from_behind(block, axis, distance):
    devices = range(lax.axis_size(axis))
    return lax.ppermute(block, axis, [(i + distance, i) for i in devices if i + distance in devices])


def inverse_rms(floats):
    return lax.rsqrt(jnp.mean(floats * floats, axis=-1, keepdims=True) + rms_epsilon)


def per_device(
    acts, norm_gain, value_grads, master, moment1, moment2, next_acts, reward_table, reward_ids
):
    micro, _, tok_dev, width = acts.shape
    kvw = value_grads.shape[3]
    toks = micro * tok_dev
    far = lax.axis_size("zhi")
    group = lax.axis_size("x") * lax.axis_size("core")
    layers_y = lax.axis_size("y")
    rows = width // (far * group)
    own_width = far * rows
    spot = lax.axis_index("x") * lax.axis_size("core") + lax.axis_index("core")
    gain = norm_gain[0]
    own_gain = lax.dynamic_index_in_dim(gain.reshape(far, group, rows), spot, 1, False)
    own_gain = own_gain.reshape(own_width)

    def by_features(block):
        parts = block.reshape(toks, far, group, rows)
        return jnp.transpose(parts, (2, 0, 1, 3)).reshape(group, toks, own_width)

    flat = acts[:, 0].reshape(toks, width)
    mine = exchange(by_features(flat), near).reshape(group * toks, own_width).astype(f32)
    inverse = inverse_rms(flat.astype(f32))
    values = value_grads[:, 0].reshape(toks, kvw).astype(f32)
    values = lax.all_gather((values * inverse).astype(bf16), near, axis=0, tiled=True)
    weights_old = lax.all_gather(master[0].astype(bf16), "zhi", axis=0, tiled=True)

    partial = jnp.einsum("td,tk->dk", mine.astype(bf16), values, preferred_element_type=f32)
    partial = (partial * own_gain[:, None]).astype(bf16)
    grad = jnp.sum(exchange(partial.reshape(far, rows, kvw), "zhi").astype(f32), axis=0)
    squares = jnp.broadcast_to(jnp.sum(grad * grad), (8, 128))
    squares = total(total(squares, ("zlo", "zhi")), ("y", "x", "core"))[0, 0]
    entries = lax.axis_size(section) * width * kvw
    rms = jnp.sqrt(squares / entries + 1e-12)
    clipped = grad * jnp.minimum(1.0, clip_level / rms)
    moment1_new = beta_first * moment1[0] + (1.0 - beta_first) * clipped
    moment2_new = beta_second * moment2[0] + (1.0 - beta_second) * clipped * clipped
    update = (
        moment1_new / bias_first / (jnp.sqrt(moment2_new / bias_second) + adam_epsilon)
        + decay_rate * master[0]
    )
    weights_new = (master[0] - learn_rate * update).astype(bf16)
    weights_new = lax.all_gather(weights_new, "zhi", axis=0, tiled=True)

    mixed = own_gain * jnp.einsum("tk,dk->td", values, weights_old, preferred_element_type=f32)
    sums = total(jnp.stack([jnp.sum(mine * mine, axis=1), jnp.sum(mine * mixed, axis=1)]), near)
    sums = sums / width
    inv = lax.rsqrt(sums[0] + rms_epsilon)[:, None]
    branch = mixed - mine * inv * (inv * sums[1][:, None])
    parts = jnp.transpose(branch.astype(bf16).reshape(group * toks, far, rows), (1, 0, 2))
    parts = exchange(parts, "y").astype(f32)
    suffix = [parts[layers_y - 1]]
    for layer in reversed(range(layers_y - 1)):
        suffix.insert(0, suffix[0] + parts[layer])
    top = suffix[0].astype(bf16)
    behind = from_behind(top, "zlo", 1).astype(f32)
    pair = (suffix[0] + behind).astype(bf16)
    behind = behind + from_behind(pair, "zlo", 2).astype(f32)
    suffix = jnp.stack([(s + behind).astype(bf16) for s in suffix])
    suffix = exchange(suffix, "y").reshape(far, group, toks, rows)
    suffix = exchange(jnp.transpose(suffix, (1, 2, 0, 3)), near)
    input_grads = jnp.transpose(suffix, (1, 2, 0, 3)).reshape(micro, 1, tok_dev, width)

    local_pos = jnp.arange(tok_dev, dtype=jnp.int32)
    first_rows = jnp.logical_and(local_pos == 0, lax.axis_index(section) == 0)
    seq_match = jnp.arange(reward_ids.shape[1], dtype=jnp.int32) == lax.axis_index(dp)
    seq_bins = jnp.sum(jnp.where(seq_match[None, :], reward_ids, 0), axis=-1)
    bin_match = (
        seq_bins[:, None] == jnp.arange(reward_table.shape[0], dtype=jnp.int32)[None, :]
    ).astype(bf16)
    embeds = jnp.dot(bin_match, reward_table, preferred_element_type=f32)
    fresh_inputs = jnp.where(
        first_rows[None, :, None], embeds[:, None, :], next_acts[:, 0].astype(f32)
    ).reshape(toks, width)
    fresh_normed = (fresh_inputs * inverse_rms(fresh_inputs) * gain).astype(bf16)
    fresh_normed = exchange(by_features(fresh_normed), near).reshape(group * toks, own_width)
    fresh = jnp.dot(fresh_normed, weights_new, preferred_element_type=f32)
    fresh = exchange(fresh.astype(bf16).reshape(group, toks, kvw), near)
    fresh = jnp.sum(fresh.astype(f32), axis=0).astype(bf16)
    fresh_values = fresh.reshape(micro, 1, tok_dev, kvw)
    return (input_grads, moment1_new[None], moment2_new[None], fresh_values)


def solution(mesh):
    fine = Mesh(mesh.devices.reshape(factors["section"] + factors["dp"]), axes)
    return jax.shard_map(
        per_device,
        mesh=fine,
        in_specs=(
            P(None, section, dp, None),
            P(section, None),
            P(None, section, dp, None),
            P(section, dp, None),
            P(section, dp, None),
            P(section, dp, None),
            P(None, section, dp, None),
            P(),
            P(),
        ),
        out_specs=(
            P(None, section, dp, None),
            P(section, dp, None),
            P(section, dp, None),
            P(None, section, dp, None),
        ),
        check_vma=False,
    )
```

```python
import jax
import jax.numpy as jnp
from jax import lax
from jax.sharding import Mesh
from jax.sharding import PartitionSpec as P

rms_epsilon = 1e-05
clip_level = 1.0
beta_first = 0.9
beta_second = 0.95
learn_rate = 0.001
decay_rate = 0.01
adam_epsilon = 1e-08
bias_first = 1.0 - 0.9**10
bias_second = 1.0 - 0.95**10

factors = {"section": (4, 4), "dp": (4, 4, 2)}
axes = ("zlo", "y", "zhi", "x", "core")
section = ("zlo", "y")
dp = ("zhi", "x", "core")
f32 = jnp.float32
bf16 = jnp.bfloat16


def exchange(blocks, axis):
    return lax.all_to_all(blocks, axis, 0, 0)


def total(value, axis):
    size = lax.axis_size(axis)
    return jnp.sum(exchange(jnp.broadcast_to(value, (size,) + value.shape), axis), axis=0)


def shifts(size):
    return sorted(range(1, size), key=lambda k: -min(k, size - k))


def by_shifts(blocks, axis):
    size = lax.axis_size(axis)
    spot = lax.axis_index(axis)
    return [
        lax.dynamic_index_in_dim(blocks, (spot + k) & (size - 1), 0, False) for k in range(size)
    ]


def shift(parts, axis):
    size = len(parts)
    came = [parts[0]] + [None] * (size - 1)
    for k in shifts(size):
        came[k] = lax.ppermute(parts[k], axis, [(i, (i + k) % size) for i in range(size)])
    return came


def swap_cores(block):
    return lax.ppermute(block, "core", [(0, 1), (1, 0)])


def sum_from_behind(block, axis):
    size = lax.axis_size(axis)
    moved = [
        lax.ppermute(block, axis, [(i + k, i) for i in range(size - k)])
        for k in range(size - 1, 0, -1)
    ]
    return sum(part.astype(f32) for part in moved)


def together(*values):
    return lax.optimization_barrier(values)


def inverse_rms(floats):
    return lax.rsqrt(jnp.mean(floats * floats, axis=-1, keepdims=True) + rms_epsilon)


def per_device(
    acts, norm_gain, value_grads, master, moment1, moment2, next_acts, reward_table, reward_ids
):
    micro, _, tok_dev, width = acts.shape
    kvw = value_grads.shape[3]
    toks = micro * tok_dev
    far = lax.axis_size("zhi")
    group = lax.axis_size("x")
    cores = lax.axis_size("core")
    layers_y = lax.axis_size("y")
    rows = width // (far * group * cores)
    strip = cores * rows
    own_width = far * strip
    core = lax.axis_index("core")
    gain = norm_gain[0]
    own_gain = lax.dynamic_index_in_dim(
        gain.reshape(far, group, strip), lax.axis_index("x"), 1, False
    ).reshape(own_width)

    def by_features(block):
        parts = block.reshape(toks, far, group, strip)
        return jnp.transpose(parts, (2, 0, 1, 3)).reshape(group, toks, own_width)

    def of_core(block, which, axis):
        shape = block.shape
        split = block.reshape(shape[:axis] + (far, cores, rows) + shape[axis + 1 :])
        split = lax.dynamic_index_in_dim(split, which, axis + 1, False)
        return split.reshape(shape[:axis] + (far * rows,) + shape[axis + 1 :])


    flat = acts[:, 0].reshape(toks, width)
    weights_old, flat = together(master[0].astype(bf16), flat)
    weights_old = lax.all_gather(weights_old, ("zhi", "core"), axis=0, tiled=True)
    mine = exchange(by_features(flat), "x").reshape(group * toks, own_width)
    inverse = inverse_rms(flat.astype(f32))
    values = value_grads[:, 0].reshape(toks, kvw).astype(f32)
    values = (values * inverse).astype(bf16)
    next_flat, values = together(next_acts[:, 0].reshape(toks, width), values)
    values = lax.all_gather(values, "x", axis=0, tiled=True)

    local_pos = jnp.arange(tok_dev, dtype=jnp.int32)
    first_rows = jnp.logical_and(local_pos == 0, lax.axis_index(section) == 0)
    seq_match = jnp.arange(reward_ids.shape[1], dtype=jnp.int32) == lax.axis_index(dp)
    seq_bins = jnp.sum(jnp.where(seq_match[None, :], reward_ids, 0), axis=-1)
    bin_match = (
        seq_bins[:, None] == jnp.arange(reward_table.shape[0], dtype=jnp.int32)[None, :]
    ).astype(bf16)
    embeds = jnp.dot(bin_match, reward_table, preferred_element_type=f32)
    fresh_inputs = jnp.where(
        first_rows[None, :, None], embeds[:, None, :], next_flat.reshape(micro, tok_dev, width).astype(f32)
    ).reshape(toks, width)
    fresh_normed = (fresh_inputs * inverse_rms(fresh_inputs) * gain).astype(bf16)
    fresh_normed, mine, values = together(by_features(fresh_normed), mine, values)
    fresh_normed = exchange(fresh_normed, "x")
    fresh_normed = fresh_normed.reshape(group * toks, own_width)

    def partial_of(which):
        part = jnp.einsum(
            "td,tk->dk", of_core(mine, which, 1), values, preferred_element_type=f32
        )
        return part * of_core(own_gain, which, 0)[:, None]

    other_part = swap_cores(partial_of(1 - core).astype(bf16))
    partial = (partial_of(core) + other_part.astype(f32)).astype(bf16).reshape(far, rows, kvw)
    partial = by_shifts(partial, "zhi")
    partial, late_values, weights_old = together(partial, values, weights_old)
    grad = sum(part.astype(f32) for part in shift(partial, "zhi"))
    squares = jnp.broadcast_to(jnp.sum(grad * grad), (8, 128))
    squares = total(squares, ("zlo", "zhi"))

    mixed = own_gain * jnp.einsum(
        "tk,dk->td", late_values, weights_old, preferred_element_type=f32
    )
    mine = mine.astype(f32)
    sums = jnp.stack([jnp.sum(mine * mine, axis=1), jnp.sum(mine * mixed, axis=1)])
    sums, fresh_normed = together(sums, fresh_normed)
    sums = total(sums, "x")
    sums = sums / width
    inv = lax.rsqrt(sums[0] + rms_epsilon)[:, None]
    branch = mixed - mine * inv * (inv * sums[1][:, None])
    parts = jnp.transpose(branch.astype(bf16).reshape(group * toks, far, strip), (1, 0, 2))
    came = [part.astype(f32) for part in shift(by_shifts(parts, "y"), "y")]
    whose = [(lax.axis_index("y") - k) & (layers_y - 1) for k in range(layers_y)]
    suffix = [
        sum(jnp.where(owner >= layer, part, 0.0) for owner, part in zip(whose, came))
        for layer in range(layers_y)
    ]
    top, squares = together(suffix[0].astype(bf16), squares)
    behind = sum_from_behind(top, "zlo")
    suffix = jnp.stack([(part + behind).astype(bf16) for part in suffix])

    squares = total(squares, ("y", "x", "core"))[0, 0]
    entries = lax.axis_size(section) * width * kvw
    rms = jnp.sqrt(squares / entries + 1e-12)
    clipped = grad * jnp.minimum(1.0, clip_level / rms)
    moment1_new = beta_first * moment1[0] + (1.0 - beta_first) * clipped
    moment2_new = beta_second * moment2[0] + (1.0 - beta_second) * clipped * clipped
    update = (
        moment1_new / bias_first / (jnp.sqrt(moment2_new / bias_second) + adam_epsilon)
        + decay_rate * master[0]
    )
    weights_new = (master[0] - learn_rate * update).astype(bf16)
    weights_new, suffix = together(weights_new, suffix)
    weights_new = lax.all_gather(weights_new, "zhi", axis=0, tiled=True)

    back = exchange(suffix.reshape(layers_y * group, toks, strip), ("y", "x"))

    weights_other = swap_cores(weights_new)
    fresh = jnp.dot(of_core(fresh_normed, core, 1), weights_new, preferred_element_type=f32)
    fresh = fresh + jnp.dot(
        of_core(fresh_normed, 1 - core, 1), weights_other, preferred_element_type=f32
    )
    fresh, back = together(fresh.astype(bf16).reshape(group, toks, kvw), back)
    fresh = exchange(fresh, "x")
    fresh = jnp.sum(fresh.astype(f32), axis=0).astype(bf16)
    fresh_values = fresh.reshape(micro, 1, tok_dev, kvw)
    input_grads = jnp.transpose(back, (1, 0, 2)).reshape(micro, 1, tok_dev, width)
    return (input_grads, moment1_new[None], moment2_new[None], fresh_values)


def solution(mesh):
    fine = Mesh(mesh.devices.reshape(factors["section"] + factors["dp"]), axes)
    return jax.shard_map(
        per_device,
        mesh=fine,
        in_specs=(
            P(None, section, dp, None),
            P(section, None),
            P(None, section, dp, None),
            P(section, dp, None),
            P(section, dp, None),
            P(section, dp, None),
            P(None, section, dp, None),
            P(),
            P(),
        ),
        out_specs=(
            P(None, section, dp, None),
            P(section, dp, None),
            P(section, dp, None),
            P(None, section, dp, None),
        ),
        check_vma=False,
    )
```

```python
import functools

import jax
import jax.numpy as jnp
from jax import lax
from jax.experimental import pallas as pl
from jax.experimental.pallas import tpu as pltpu
from jax.sharding import Mesh
from jax.sharding import PartitionSpec as P

rms_epsilon = 1e-05
clip_level = 1.0
beta_first = 0.9
beta_second = 0.95
learn_rate = 0.001
decay_rate = 0.01
adam_epsilon = 1e-08
bias_first = 1.0 - 0.9**10
bias_second = 1.0 - 0.95**10

factors = {"section": (4, 4), "dp": (4, 4, 2)}
axes = ("zlo", "y", "zhi", "x", "core")
section = ("zlo", "y")
dp = ("zhi", "x", "core")
f32 = jnp.float32
bf16 = jnp.bfloat16


def exchange(blocks, axis):
    return lax.all_to_all(blocks, axis, 0, 0)


def total(value, axis):
    return jnp.sum(exchange(value, axis), axis=0)


def shifts(size):
    return sorted(range(1, size), key=lambda k: -min(k, size - k))


def shift(parts, axis):
    size = len(parts)
    came = [parts[0]] + [None] * (size - 1)
    for k in shifts(size):
        came[k] = lax.ppermute(parts[k], axis, [(i, (i + k) % size) for i in range(size)])
    return came


def swap_cores(block):
    return lax.ppermute(block, "core", [(0, 1), (1, 0)])


def sum_from_behind(block, axis):
    size = lax.axis_size(axis)
    moved = [
        lax.ppermute(block, axis, [(i + k, i) for i in range(size - k)])
        for k in range(size - 1, 0, -1)
    ]
    return sum(part.astype(f32) for part in moved)


def together(*values):
    return lax.optimization_barrier(values)


def inverse_rms(floats):
    return lax.rsqrt(jnp.mean(floats * floats, axis=-1, keepdims=True) + rms_epsilon)


def local(kernel, out_shapes, spots, *arrays, flops=0):
    moved = sum(a.size * a.dtype.itemsize for a in arrays)
    moved += sum(s.size * s.dtype.itemsize for s in out_shapes)
    return pl.pallas_call(
        kernel,
        out_shape=out_shapes,
        in_specs=[pl.BlockSpec(memory_space=pltpu.SMEM)]
        + [pl.BlockSpec(memory_space=pltpu.VMEM)] * len(arrays),
        out_specs=[pl.BlockSpec(memory_space=pltpu.VMEM)] * len(out_shapes),
        compiler_params=pltpu.CompilerParams(vmem_limit_bytes=48 * 1024 * 1024),
        cost_estimate=pl.CostEstimate(flops=0, bytes_accessed=0, transcendentals=0),
    )(spots, *arrays)


def strip_at(start, rows):
    return pl.ds(pl.multiple_of(start, rows), rows)


def split_kernel(sizes, spots, acts, values, out):
    far, group, cores, rows = sizes
    core = spots[0]
    half = far * rows
    floats = acts[...].astype(f32)
    scaled = (values[...].astype(f32) * inverse_rms(floats)).astype(bf16)
    for x in range(group):
        for z in range(far):
            for c in range(cores):
                start = ((z * group + x) * cores + ((core + c) & (cores - 1))) * rows
                out[x, :, c * half + z * rows : c * half + (z + 1) * rows] = acts[
                    :, strip_at(start, rows)
                ]
        out[x, :, cores * half :] = scaled


def other_kernel(half, spots, mine, gain, out):
    left = mine[:, half : 2 * half]
    part = lax.dot_general(
        left, mine[:, 2 * half :], (((0,), (0,)), ((), ())), preferred_element_type=f32
    )
    out[...] = (part * gain[...]).astype(bf16)


def own_kernel(half, spots, mine, gain, came, out):
    part = lax.dot_general(
        mine[:, :half], mine[:, 2 * half :], (((0,), (0,)), ((), ())), preferred_element_type=f32
    )
    out[...] = (part * gain[...] + came[...].astype(f32)).astype(bf16)


def upstream_kernel(half, spots, mine, own, other, gain, mixed, sums):
    values = mine[:, 2 * half :]
    squares, products = 0.0, 0.0
    for c, weights in enumerate((own, other)):
        cols = slice(c * half, (c + 1) * half)
        part = lax.dot_general(
            values, weights[...], (((1,), (1,)), ((), ())), preferred_element_type=f32
        )
        part = part * gain[:, cols]
        mixed[:, cols] = part
        floats = mine[:, cols].astype(f32)
        squares = squares + jnp.sum(floats * floats, axis=1, keepdims=True)
        products = products + jnp.sum(floats * part, axis=1, keepdims=True)
    lane = lax.broadcasted_iota(jnp.int32, (mine.shape[0], 128), 1)
    both = jnp.where(lane == 0, squares, jnp.where(lane == 1, products, 0.0))
    for x in range(sums.shape[0]):
        sums[x] = both.T[:8]


def branch_kernel(sizes, spots, mine, mixed, sums, *outs):
    far, rows, width = sizes
    half = far * rows
    both = jnp.concatenate([jnp.sum(sums[...], axis=0)] * 16, axis=0).T
    inv = lax.rsqrt(both[:, 0:1] / width + rms_epsilon)
    pull = inv * (inv * (both[:, 1:2] / width))
    for k, out in enumerate(outs):
        z = (spots[1] + k) & (far - 1)
        for c in range(2):
            cols = strip_at(c * half + z * rows, rows)
            block = mixed[:, cols] - mine[:, cols].astype(f32) * pull
            out[:, c * rows : (c + 1) * rows] = block.astype(bf16)


def fresh_kernel(sizes, ids_shape, spots, acts, gain, table, out):
    far, group, cores, rows = sizes
    micro, seqs = ids_shape
    core = spots[0]
    half = far * rows
    floats = acts[...].astype(f32)
    toks = floats.shape[0]
    row = lax.broadcasted_iota(jnp.int32, (toks, 1), 0)
    for m in range(micro):
        bin_id = spots[4 + m * seqs + spots[3]]
        embed = jnp.zeros((1, floats.shape[1]), f32)
        for b in range(table.shape[0]):
            embed = jnp.where(bin_id == b, table[b : b + 1, :].astype(f32), embed)
        first = jnp.logical_and(row == m * (toks // micro), spots[2] == 0)
        floats = jnp.where(first, embed, floats)
    inverse = inverse_rms(floats)
    normed = (floats * inverse * gain[...]).astype(bf16)
    for x in range(group):
        for z in range(far):
            start = (z * group + x) * cores * rows
            for c in range(cores):
                place = ((core + c) & (cores - 1)) * half + z * rows
                block = normed[:, start + c * rows : start + (c + 1) * rows]
                out[x, :, strip_at(place, rows)] = block


def join_kernel(rows, spots, back, out):
    cores = back.shape[2] // rows
    for j in range(back.shape[0]):
        for c in range(cores):
            start = (j * cores + ((spots[0] + c) & (cores - 1))) * rows
            out[:, strip_at(start, rows)] = back[j, :, c * rows : (c + 1) * rows]


def per_device(
    acts, norm_gain, value_grads, master, moment1, moment2, next_acts, reward_table, reward_ids
):
    micro, _, tok_dev, width = acts.shape
    kvw = value_grads.shape[3]
    toks = micro * tok_dev
    far = lax.axis_size("zhi")
    group = lax.axis_size("x")
    cores = lax.axis_size("core")
    layers_y = lax.axis_size("y")
    rows = width // (far * group * cores)
    half = far * rows
    all_toks = group * toks
    core, spot_y, spot_x = (lax.axis_index(name) for name in ("core", "y", "x"))
    spots = jnp.stack([core, spot_y, lax.axis_index(section), lax.axis_index(dp)])
    spots = jnp.concatenate([spots, reward_ids.reshape(-1)])
    shape = jax.ShapeDtypeStruct
    gain = norm_gain[0]

    def of_features(block):
        split = block.reshape(block.shape[:-1] + (far, group, cores, rows))
        split = lax.dynamic_index_in_dim(split, spot_x, split.ndim - 3, False)
        halves = [
            lax.dynamic_index_in_dim(split, core ^ c, split.ndim - 2, False) for c in range(cores)
        ]
        return jnp.concatenate([h.reshape(block.shape[:-1] + (half,)) for h in halves], axis=-1)

    own_gain = of_features(gain)

    flat = acts[:, 0].reshape(toks, width)
    blocks = local(
        functools.partial(split_kernel, (far, group, cores, rows)),
        [shape((group, toks, cores * half + kvw), bf16)],
        spots,
        flat,
        value_grads[:, 0].reshape(toks, kvw),
    )[0]
    weights_old, blocks = together(master[0].astype(bf16), blocks)
    mine = exchange(blocks, "x").reshape(all_toks, cores * half + kvw)
    weights_old = lax.all_gather(weights_old, "zhi", axis=0, tiled=True)
    mine, weights_old = together(mine, weights_old)
    weights_other = swap_cores(weights_old)

    flops = 2 * all_toks * half * kvw
    other = local(
        functools.partial(other_kernel, half),
        [shape((half, kvw), bf16)],
        spots,
        mine,
        own_gain[half:, None],
        flops=flops,
    )[0]
    partial = local(
        functools.partial(own_kernel, half),
        [shape((half, kvw), bf16)],
        spots,
        mine,
        own_gain[:half, None],
        swap_cores(other),
        flops=flops,
    )[0]
    partial, weights_other = together(partial, weights_other)
    grad = lax.psum_scatter(partial, "zhi", scatter_dimension=0, tiled=True).astype(f32)

    mixed, sums = local(
        functools.partial(upstream_kernel, half),
        [shape((all_toks, cores * half), f32), shape((group, 8, all_toks), f32)],
        spots,
        mine,
        weights_old,
        weights_other,
        own_gain[None],
        flops=2 * flops,
    )
    sums = exchange(sums, "x")
    parts = local(
        functools.partial(branch_kernel, (far, rows, width)),
        [shape((all_toks, cores * rows), bf16)] * layers_y,
        spots,
        mine,
        mixed,
        sums,
    )
    came = [part.astype(f32) for part in shift(parts, "y")]
    whose = [(spot_y - k) & (layers_y - 1) for k in range(layers_y)]
    suffix = [
        sum(jnp.where(owner >= layer, part, 0.0) for owner, part in zip(whose, came))
        for layer in range(layers_y)
    ]

    next_flat, parts = together(next_acts[:, 0].reshape(toks, width), parts)
    fresh_normed = local(
        functools.partial(fresh_kernel, (far, group, cores, rows), reward_ids.shape),
        [shape((group, toks, cores * half), bf16)],
        spots,
        next_flat,
        norm_gain,
        reward_table,
    )[0]
    fresh_normed = exchange(fresh_normed, "x").reshape(all_toks, cores * half)

    squares = jnp.broadcast_to(jnp.sum(grad * grad), (lax.axis_size(("zlo","zhi")), 8, 128))
    top, squares, fresh_normed = together(suffix[0].astype(bf16), squares, fresh_normed)
    squares = total(squares, ("zlo", "zhi"))
    behind = sum_from_behind(top, "zlo")
    suffix = jnp.stack([(part + behind).astype(bf16) for part in suffix])
    squares = total(jnp.broadcast_to(squares, (lax.axis_size(("y","x","core")), 8, 128)), ("y", "x", "core"))[0, 0]
    entries = lax.axis_size(section) * width * kvw
    rms = jnp.sqrt(squares / entries + 1e-12)
    clipped = grad * jnp.minimum(1.0, clip_level / rms)
    moment1_new = beta_first * moment1[0] + (1.0 - beta_first) * clipped
    moment2_new = beta_second * moment2[0] + (1.0 - beta_second) * clipped * clipped
    update = (
        moment1_new / bias_first / (jnp.sqrt(moment2_new / bias_second) + adam_epsilon)
        + decay_rate * master[0]
    )
    weights_new = (master[0] - learn_rate * update).astype(bf16)
    weights_new, suffix = together(weights_new, suffix)
    weights_new = lax.all_gather(weights_new, "zhi", axis=0, tiled=True)
    strip = cores * rows
    back = exchange(suffix.reshape(layers_y * group, toks, strip), ("y", "x"))

    fresh = jnp.dot(fresh_normed[:, :half], weights_new, preferred_element_type=f32)
    fresh = fresh + jnp.dot(
        fresh_normed[:, half:], swap_cores(weights_new), preferred_element_type=f32
    )
    fresh, back = together(fresh.astype(bf16).reshape(group, toks, kvw), back)
    fresh = jnp.sum(exchange(fresh, "x").astype(f32), axis=0).astype(bf16)
    fresh_values = fresh.reshape(micro, 1, tok_dev, kvw)

    input_grads = local(
        functools.partial(join_kernel, rows), [shape((toks, width), bf16)], spots, back
    )[0].reshape(micro, 1, tok_dev, width)
    return (input_grads, moment1_new[None], moment2_new[None], fresh_values)


def solution(mesh):
    fine = Mesh(mesh.devices.reshape(factors["section"] + factors["dp"]), axes)
    return jax.shard_map(
        per_device,
        mesh=fine,
        in_specs=(
            P(None, section, dp, None),
            P(section, None),
            P(None, section, dp, None),
            P(section, dp, None),
            P(section, dp, None),
            P(section, dp, None),
            P(None, section, dp, None),
            P(),
            P(),
        ),
        out_specs=(
            P(None, section, dp, None),
            P(section, dp, None),
            P(section, dp, None),
            P(None, section, dp, None),
        ),
        check_vma=False,
    )
```

```python
import functools

import jax
import jax.numpy as jnp
from jax import lax
from jax.experimental import pallas as pl
from jax.experimental.pallas import tpu as pltpu
from jax.sharding import Mesh
from jax.sharding import PartitionSpec as P

rms_epsilon = 1e-05
clip_level = 1.0
beta_first = 0.9
beta_second = 0.95
learn_rate = 0.001
decay_rate = 0.01
adam_epsilon = 1e-08
bias_first = 1.0 - 0.9**10
bias_second = 1.0 - 0.95**10

factors = {"section": (4, 4), "dp": (4, 4, 2)}
axes = ("zlo", "y", "zhi", "x", "core")
section = ("zlo", "y")
dp = ("zhi", "x", "core")
heavy = 2 * 10**10
f32 = jnp.float32
bf16 = jnp.bfloat16


def exchange(blocks, axis):
    return lax.all_to_all(blocks, axis, 0, 0)


def shifts(size):
    return sorted(range(1, size), key=lambda k: -min(k, size - k))


def shift(parts, axis):
    size = len(parts)
    came = [parts[0]] + [None] * (size - 1)
    for k in shifts(size):
        came[k] = lax.ppermute(parts[k], axis, [(i, (i + k) % size) for i in range(size)])
    return came


def swap_cores(block):
    return lax.ppermute(block, "core", [(0, 1), (1, 0)])


def from_behind(block, axis):
    size = lax.axis_size(axis)
    return [
        lax.ppermute(block, axis, [(i + k, i) for i in range(size - k)])
        for k in range(size - 1, 0, -1)
    ]


def together(*values):
    return lax.optimization_barrier(values)


def inverse_rms(floats):
    return lax.rsqrt(jnp.mean(floats * floats, axis=-1, keepdims=True) + rms_epsilon)


def local(kernel, out_shapes, spots, *arrays, weight=0):
    return pl.pallas_call(
        kernel,
        out_shape=out_shapes,
        in_specs=[pl.BlockSpec(memory_space=pltpu.SMEM)]
        + [pl.BlockSpec(memory_space=pltpu.VMEM)] * len(arrays),
        out_specs=[pl.BlockSpec(memory_space=pltpu.VMEM)] * len(out_shapes),
        compiler_params=pltpu.CompilerParams(vmem_limit_bytes=48 * 1024 * 1024),
        cost_estimate=pl.CostEstimate(flops=weight, bytes_accessed=0, transcendentals=0),
    )(spots, *arrays)


def strip_at(start, rows):
    return pl.ds(pl.multiple_of(start, rows), rows)


def split_kernel(sizes, spots, acts, values, out):
    far, group, cores, rows = sizes
    core = spots[0]
    half = far * rows
    floats = acts[...].astype(f32)
    scaled = (values[...].astype(f32) * inverse_rms(floats)).astype(bf16)
    for x in range(group):
        for z in range(far):
            for c in range(cores):
                start = ((z * group + x) * cores + ((core + c) & (cores - 1))) * rows
                out[x, :, c * half + z * rows : c * half + (z + 1) * rows] = acts[
                    :, strip_at(start, rows)
                ]
        out[x, :, cores * half :] = scaled


def other_kernel(half, spots, mine, gain, out):
    left = mine[:, half : 2 * half]
    part = lax.dot_general(
        left, mine[:, 2 * half :], (((0,), (0,)), ((), ())), preferred_element_type=f32
    )
    out[...] = (part * gain[...]).astype(bf16)


def own_kernel(half, spots, mine, gain, came, out):
    part = lax.dot_general(
        mine[:, :half], mine[:, 2 * half :], (((0,), (0,)), ((), ())), preferred_element_type=f32
    )
    out[...] = (part * gain[...] + came[...].astype(f32)).astype(bf16)


def upstream_kernel(half, spots, mine, own, other, gain, mixed, sums):
    values = mine[:, 2 * half :]
    squares, products = 0.0, 0.0
    for c, weights in enumerate((own, other)):
        cols = slice(c * half, (c + 1) * half)
        part = lax.dot_general(
            values, weights[...], (((1,), (1,)), ((), ())), preferred_element_type=f32
        )
        part = part * gain[:, cols]
        mixed[:, cols] = part
        floats = mine[:, cols].astype(f32)
        squares = squares + jnp.sum(floats * floats, axis=1, keepdims=True)
        products = products + jnp.sum(floats * part, axis=1, keepdims=True)
    lane = lax.broadcasted_iota(jnp.int32, (mine.shape[0], 128), 1)
    both = jnp.where(lane == 0, squares, jnp.where(lane == 1, products, 0.0))
    for x in range(sums.shape[0]):
        sums[x] = both.T[:8]


def branch_kernel(sizes, spots, mine, mixed, sums, *outs):
    far, rows, width = sizes
    half = far * rows
    both = jnp.concatenate([jnp.sum(sums[...], axis=0)] * 16, axis=0).T
    inv = lax.rsqrt(both[:, 0:1] / width + rms_epsilon)
    pull = inv * (inv * (both[:, 1:2] / width))
    for k, out in enumerate(outs):
        z = (spots[1] + k) & (far - 1)
        for c in range(2):
            cols = strip_at(c * half + z * rows, rows)
            block = mixed[:, cols] - mine[:, cols].astype(f32) * pull
            out[:, c * rows : (c + 1) * rows] = block.astype(bf16)


def fresh_kernel(sizes, ids_shape, spots, acts, gain, table, out):
    far, group, cores, rows = sizes
    micro, seqs = ids_shape
    core = spots[0]
    half = far * rows
    floats = acts[...].astype(f32)
    toks = floats.shape[0]
    row = lax.broadcasted_iota(jnp.int32, (toks, 1), 0)
    for m in range(micro):
        bin_id = spots[4 + m * seqs + spots[3]]
        embed = jnp.zeros((1, floats.shape[1]), f32)
        for b in range(table.shape[0]):
            embed = jnp.where(bin_id == b, table[b : b + 1, :].astype(f32), embed)
        first = jnp.logical_and(row == m * (toks // micro), spots[2] == 0)
        floats = jnp.where(first, embed, floats)
    inverse = inverse_rms(floats)
    normed = (floats * inverse * gain[...]).astype(bf16)
    for x in range(group):
        for z in range(far):
            start = (z * group + x) * cores * rows
            for c in range(cores):
                place = ((core + c) & (cores - 1)) * half + z * rows
                block = normed[:, start + c * rows : start + (c + 1) * rows]
                out[x, :, strip_at(place, rows)] = block


def top_kernel(spots, *refs):
    *came, out = refs
    out[...] = sum(part[...].astype(f32) for part in came).astype(bf16)


def suffix_kernel(layers, group, spots, *refs):
    *parts, out = refs
    came = [part[...].astype(f32) for part in parts[:layers]]
    behind = sum(part[...].astype(f32) for part in parts[layers:])
    toks = out.shape[1]
    for layer in range(layers):
        block = behind
        for k in range(layers):
            here = ((spots[1] - k) & (layers - 1)) >= layer
            block = block + jnp.where(here, came[k], 0.0)
        for x in range(group):
            out[layer * group + x] = block[x * toks : (x + 1) * toks].astype(bf16)


def squares_kernel(spots, grad, out):
    floats = grad[...].astype(f32)
    out[...] = jnp.broadcast_to(jnp.sum(floats * floats), out.shape)


def relay_kernel(spots, sums, out):
    out[...] = jnp.broadcast_to(jnp.sum(sums[...], axis=0, keepdims=True), out.shape)


def adam_kernel(entries, spots, sums, grad, master, first, second, first_new, second_new, weights):
    squares = jnp.sum(sums[...], axis=0)
    clip = jnp.minimum(1.0, clip_level / jnp.sqrt(squares / entries + 1e-12))[0:1, 0:1]
    clipped = grad[...].astype(f32) * clip
    moment1 = beta_first * first[...] + (1.0 - beta_first) * clipped
    moment2 = beta_second * second[...] + (1.0 - beta_second) * clipped * clipped
    first_new[...] = moment1
    second_new[...] = moment2
    update = (
        moment1 / bias_first / (jnp.sqrt(moment2 / bias_second) + adam_epsilon)
        + decay_rate * master[...]
    )
    weights[...] = (master[...] - learn_rate * update).astype(bf16)


def join_kernel(rows, spots, back, out):
    cores = back.shape[2] // rows
    for j in range(back.shape[0]):
        for c in range(cores):
            start = (j * cores + ((spots[0] + c) & (cores - 1))) * rows
            out[:, strip_at(start, rows)] = back[j, :, c * rows : (c + 1) * rows]


def per_device(
    acts, norm_gain, value_grads, master, moment1, moment2, next_acts, reward_table, reward_ids
):
    micro, _, tok_dev, width = acts.shape
    kvw = value_grads.shape[3]
    toks = micro * tok_dev
    far = lax.axis_size("zhi")
    group = lax.axis_size("x")
    cores = lax.axis_size("core")
    layers_y = lax.axis_size("y")
    rows = width // (far * group * cores)
    half = far * rows
    all_toks = group * toks
    core, spot_y, spot_x = (lax.axis_index(name) for name in ("core", "y", "x"))
    spots = jnp.stack([core, spot_y, lax.axis_index(section), lax.axis_index(dp)])
    spots = jnp.concatenate([spots, reward_ids.reshape(-1)])
    shape = jax.ShapeDtypeStruct
    gain = norm_gain[0]

    def of_features(block):
        split = block.reshape(block.shape[:-1] + (far, group, cores, rows))
        split = lax.dynamic_index_in_dim(split, spot_x, split.ndim - 3, False)
        halves = [
            lax.dynamic_index_in_dim(split, core ^ c, split.ndim - 2, False) for c in range(cores)
        ]
        return jnp.concatenate([h.reshape(block.shape[:-1] + (half,)) for h in halves], axis=-1)

    own_gain = of_features(gain)

    flat = acts[:, 0].reshape(toks, width)
    blocks = local(
        functools.partial(split_kernel, (far, group, cores, rows)),
        [shape((group, toks, cores * half + kvw), bf16)],
        spots,
        flat,
        value_grads[:, 0].reshape(toks, kvw),
    )[0]
    weights_old, blocks = together(master[0].astype(bf16), blocks)
    mine = exchange(blocks, "x").reshape(all_toks, cores * half + kvw)
    weights_old = lax.all_gather(weights_old, "zhi", axis=0, tiled=True)
    mine, weights_old = together(mine, weights_old)

    other = local(
        functools.partial(other_kernel, half),
        [shape((half, kvw), bf16)],
        spots,
        mine,
        own_gain[half:, None],
    )[0]
    partial = local(
        functools.partial(own_kernel, half),
        [shape((half, kvw), bf16)],
        spots,
        mine,
        own_gain[:half, None],
        swap_cores(other),
    )[0]
    partial, weights_old = together(partial, weights_old)
    grad = lax.psum_scatter(partial, "zhi", scatter_dimension=0, tiled=True)
    weights_other = swap_cores(weights_old)

    mixed, sums = local(
        functools.partial(upstream_kernel, half),
        [shape((all_toks, cores * half), f32), shape((group, 8, all_toks), f32)],
        spots,
        mine,
        weights_old,
        weights_other,
        own_gain[None],
    )
    sums = exchange(sums, "x")
    parts = local(
        functools.partial(branch_kernel, (far, rows, width)),
        [shape((all_toks, cores * rows), bf16)] * layers_y,
        spots,
        mine,
        mixed,
        sums,
    )
    came = shift(parts, "y")
    top_shape = shape((all_toks, cores * rows), bf16)
    top = local(top_kernel, [top_shape], spots, *came)[0]

    next_flat, parts = together(next_acts[:, 0].reshape(toks, width), parts)
    fresh_normed = local(
        functools.partial(fresh_kernel, (far, group, cores, rows), reward_ids.shape),
        [shape((group, toks, cores * half), bf16)],
        spots,
        next_flat,
        norm_gain,
        reward_table,
    )[0]
    fresh_normed = exchange(fresh_normed, "x").reshape(all_toks, cores * half)

    near = ("y", "x", "core")
    along = ("zlo", "zhi")
    tile = (8, 128)
    squares = local(
        squares_kernel, [shape((lax.axis_size(near),) + tile, f32)], spots, grad, weight=heavy
    )[0]
    top, squares, fresh_normed = together(top, squares, fresh_normed)
    behind = from_behind(top, "zlo")
    squares = exchange(squares, near)
    squares = local(relay_kernel, [shape((lax.axis_size(along),) + tile, f32)], spots, squares)[0]
    squares = exchange(squares, along)
    shard = shape((rows, kvw), f32)
    moment1_new, moment2_new, weights_new = local(
        functools.partial(adam_kernel, lax.axis_size(section) * width * kvw),
        [shard, shard, shape((rows, kvw), bf16)],
        spots,
        squares,
        grad,
        master[0],
        moment1[0],
        moment2[0],
    )
    suffix = local(
        functools.partial(suffix_kernel, layers_y, group),
        [shape((layers_y * group, toks, cores * rows), bf16)],
        spots,
        *came,
        *behind,
    )[0]
    weights_new, suffix = together(weights_new, suffix)
    weights_new = lax.all_gather(weights_new, "zhi", axis=0, tiled=True)
    back = exchange(suffix, ("y", "x"))

    fresh = jnp.dot(fresh_normed[:, :half], weights_new, preferred_element_type=f32)
    fresh = fresh + jnp.dot(
        fresh_normed[:, half:], swap_cores(weights_new), preferred_element_type=f32
    )
    fresh, back = together(fresh.astype(bf16).reshape(group, toks, kvw), back)
    fresh = jnp.sum(exchange(fresh, "x").astype(f32), axis=0).astype(bf16)
    fresh_values = fresh.reshape(micro, 1, tok_dev, kvw)

    input_grads = local(
        functools.partial(join_kernel, rows), [shape((toks, width), bf16)], spots, back
    )[0].reshape(micro, 1, tok_dev, width)
    return (input_grads, moment1_new[None], moment2_new[None], fresh_values)


def solution(mesh):
    fine = Mesh(mesh.devices.reshape(factors["section"] + factors["dp"]), axes)
    return jax.shard_map(
        per_device,
        mesh=fine,
        in_specs=(
            P(None, section, dp, None),
            P(section, None),
            P(None, section, dp, None),
            P(section, dp, None),
            P(section, dp, None),
            P(section, dp, None),
            P(None, section, dp, None),
            P(),
            P(),
        ),
        out_specs=(
            P(None, section, dp, None),
            P(section, dp, None),
            P(section, dp, None),
            P(None, section, dp, None),
        ),
        check_vma=False,
    )
```

```python
import functools

import jax
import jax.numpy as jnp
from jax import lax
from jax.experimental import pallas as pl
from jax.experimental.pallas import tpu as pltpu
from jax.sharding import Mesh
from jax.sharding import PartitionSpec as P

rms_epsilon = 1e-05
clip_level = 1.0
beta_first = 0.9
beta_second = 0.95
learn_rate = 0.001
decay_rate = 0.01
adam_epsilon = 1e-08
bias_first = 1.0 - 0.9**10
bias_second = 1.0 - 0.95**10

factors = {"section": (4, 4), "dp": (4, 4, 2)}
axes = ("zlo", "y", "zhi", "x", "core")
section = ("zlo", "y")
dp = ("zhi", "x", "core")
heavy = 2 * 10**10
f32 = jnp.float32
bf16 = jnp.bfloat16


def exchange(blocks, axis):
    return lax.all_to_all(blocks, axis, 0, 0)


def shifts(size):
    return sorted(range(1, size), key=lambda k: -min(k, size - k))


def shift(parts, axis):
    size = len(parts)
    came = [parts[0]] + [None] * (size - 1)
    for k in shifts(size):
        came[k] = lax.ppermute(parts[k], axis, [(i, (i + k) % size) for i in range(size)])
    return came


def swap_cores(block):
    return lax.ppermute(block, "core", [(0, 1), (1, 0)])


def from_behind(block, axis, distance):
    size = lax.axis_size(axis)
    return lax.ppermute(block, axis, [(i + distance, i) for i in range(size - distance)])


def together(*values):
    return lax.optimization_barrier(values)


def inverse_rms(floats):
    return lax.rsqrt(jnp.mean(floats * floats, axis=-1, keepdims=True) + rms_epsilon)


def local(kernel, out_shapes, spots, *arrays, weight=0, scratch=(), after=()):
    def body(spots, *refs):
        kernel(spots, *refs[: len(arrays)], *refs[len(arrays) + len(after) :])

    return pl.pallas_call(
        body,
        out_shape=out_shapes,
        in_specs=[pl.BlockSpec(memory_space=pltpu.SMEM)]
        + [pl.BlockSpec(memory_space=pltpu.VMEM)] * len(arrays)
        + [pl.BlockSpec(memory_space=pl.ANY)] * len(after),
        out_specs=[pl.BlockSpec(memory_space=pltpu.VMEM)] * len(out_shapes),
        scratch_shapes=scratch,
        compiler_params=pltpu.CompilerParams(vmem_limit_bytes=48 * 1024 * 1024),
        cost_estimate=pl.CostEstimate(flops=weight, bytes_accessed=0, transcendentals=0),
    )(spots, *arrays, *after)


def strip_at(start, rows):
    return pl.ds(pl.multiple_of(start, rows), rows)


def split_kernel(sizes, spots, acts, values, out):
    far, group, cores, rows = sizes
    core = spots[0]
    half = far * rows
    floats = acts[...].astype(f32)
    scaled = (values[...].astype(f32) * inverse_rms(floats)).astype(bf16)
    for x in range(group):
        for z in range(far):
            for c in range(cores):
                start = ((z * group + x) * cores + ((core + c) & (cores - 1))) * rows
                out[x, :, c * half + z * rows : c * half + (z + 1) * rows] = acts[
                    :, strip_at(start, rows)
                ]
        out[x, :, cores * half :] = scaled


def other_kernel(half, spots, mine, gain, out):
    left = mine[:, half : 2 * half]
    part = lax.dot_general(
        left, mine[:, 2 * half :], (((0,), (0,)), ((), ())), preferred_element_type=f32
    )
    out[...] = (part * gain[...]).astype(bf16)


def own_kernel(half, spots, mine, gain, came, out):
    part = lax.dot_general(
        mine[:, :half], mine[:, 2 * half :], (((0,), (0,)), ((), ())), preferred_element_type=f32
    )
    out[...] = (part * gain[...] + came[...].astype(f32)).astype(bf16)


def upstream_kernel(half, spots, mine, own, other, gain, mixed, sums):
    values = mine[:, 2 * half :]
    squares, products = 0.0, 0.0
    for c, weights in enumerate((own, other)):
        cols = slice(c * half, (c + 1) * half)
        part = lax.dot_general(
            values, weights[...], (((1,), (1,)), ((), ())), preferred_element_type=f32
        )
        part = part * gain[:, cols]
        mixed[:, cols] = part
        floats = mine[:, cols].astype(f32)
        squares = squares + jnp.sum(floats * floats, axis=1, keepdims=True)
        products = products + jnp.sum(floats * part, axis=1, keepdims=True)
    lane = lax.broadcasted_iota(jnp.int32, (mine.shape[0], 128), 1)
    both = jnp.where(lane == 0, squares, jnp.where(lane == 1, products, 0.0))
    for x in range(sums.shape[0]):
        sums[x] = both.T[:8]


def branch_kernel(sizes, spots, mine, mixed, sums, out):
    far, rows, width = sizes
    half = far * rows
    both = jnp.concatenate([jnp.sum(sums[...], axis=0)] * 16, axis=0).T
    inv = lax.rsqrt(both[:, 0:1] / width + rms_epsilon)
    pull = inv * (inv * (both[:, 1:2] / width))
    for z in range(far):
        for c in range(mixed.shape[1] // half):
            cols = slice(c * half + z * rows, c * half + (z + 1) * rows)
            block = mixed[:, cols] - mine[:, cols].astype(f32) * pull
            out[z, :, c * rows : (c + 1) * rows] = block.astype(bf16)


def fresh_kernel(sizes, ids_shape, spots, acts, gain, table, *refs):
    *outs, normed = refs
    far, group, cores, rows = sizes
    micro, seqs = ids_shape
    half = far * rows
    floats = acts[...].astype(f32)
    toks = floats.shape[0]
    row = lax.broadcasted_iota(jnp.int32, (toks, 1), 0)
    for m in range(micro):
        bin_id = spots[5 + m * seqs + spots[3]]
        embed = jnp.zeros((1, floats.shape[1]), f32)
        for b in range(table.shape[0]):
            embed = jnp.where(bin_id == b, table[b : b + 1, :].astype(f32), embed)
        first = jnp.logical_and(row == m * (toks // micro), spots[2] == 0)
        floats = jnp.where(first, embed, floats)
    normed[...] = (floats * inverse_rms(floats) * gain[...]).astype(bf16)
    for k, out in enumerate(outs):
        x = (spots[4] + k) & (group - 1)
        for z in range(far):
            for c in range(cores):
                start = ((z * group + x) * cores + ((spots[0] + c) & (cores - 1))) * rows
                out[:, c * half + z * rows : c * half + (z + 1) * rows] = normed[
                    :, strip_at(start, rows)
                ]


def values_kernel(half, spots, *refs):
    *blocks, own, other, out = refs
    group = len(blocks)
    for k, block in enumerate(blocks):
        part = jnp.dot(block[:, :half], own[...], preferred_element_type=f32)
        part = part + jnp.dot(block[:, half:], other[...], preferred_element_type=f32)
        out[(spots[4] - k) & (group - 1)] = part.astype(bf16)


def top_kernel(spots, came, out):
    out[...] = jnp.sum(came[...].astype(f32), axis=0).astype(bf16)


def pair_kernel(spots, top, behind, out):
    out[...] = (top[...].astype(f32) + behind[...].astype(f32)).astype(bf16)


def suffix_kernel(group, spots, came, *refs):
    *parts, out = refs
    block = sum(part[...].astype(f32) for part in parts)
    toks = out.shape[1]
    for layer in reversed(range(came.shape[0])):
        block = block + came[layer].astype(f32)
        for x in range(group):
            out[layer * group + x] = block[x * toks : (x + 1) * toks].astype(bf16)


def squares_kernel(spots, grad, out):
    floats = grad[...].astype(f32)
    out[...] = jnp.broadcast_to(jnp.sum(floats * floats), out.shape)


def relay_kernel(spots, sums, out):
    out[...] = jnp.broadcast_to(jnp.sum(sums[...], axis=0, keepdims=True), out.shape)


def adam_kernel(entries, spots, sums, grad, master, first, second, first_new, second_new, weights):
    squares = jnp.sum(sums[...], axis=0)
    clip = jnp.minimum(1.0, clip_level / jnp.sqrt(squares / entries + 1e-12))[0:1, 0:1]
    clipped = grad[...].astype(f32) * clip
    moment1 = beta_first * first[...] + (1.0 - beta_first) * clipped
    moment2 = beta_second * second[...] + (1.0 - beta_second) * clipped * clipped
    first_new[...] = moment1
    second_new[...] = moment2
    update = (
        moment1 / bias_first / (jnp.sqrt(moment2 / bias_second) + adam_epsilon)
        + decay_rate * master[...]
    )
    weights[...] = (master[...] - learn_rate * update).astype(bf16)


def join_kernel(rows, spots, back, out):
    cores = back.shape[2] // rows
    for j in range(back.shape[0]):
        for c in range(cores):
            start = (j * cores + ((spots[0] + c) & (cores - 1))) * rows
            out[:, strip_at(start, rows)] = back[j, :, c * rows : (c + 1) * rows]


def per_device(
    acts, norm_gain, value_grads, master, moment1, moment2, next_acts, reward_table, reward_ids
):
    micro, _, tok_dev, width = acts.shape
    kvw = value_grads.shape[3]
    toks = micro * tok_dev
    far = lax.axis_size("zhi")
    group = lax.axis_size("x")
    cores = lax.axis_size("core")
    layers_y = lax.axis_size("y")
    rows = width // (far * group * cores)
    half = far * rows
    all_toks = group * toks
    core, spot_y, spot_x = (lax.axis_index(name) for name in ("core", "y", "x"))
    spots = jnp.stack([core, spot_y, lax.axis_index(section), lax.axis_index(dp), spot_x])
    spots = jnp.concatenate([spots, reward_ids.reshape(-1)])
    shape = jax.ShapeDtypeStruct
    gain = norm_gain[0]

    def of_features(block):
        split = block.reshape(block.shape[:-1] + (far, group, cores, rows))
        split = lax.dynamic_index_in_dim(split, spot_x, split.ndim - 3, False)
        halves = [
            lax.dynamic_index_in_dim(split, core ^ c, split.ndim - 2, False) for c in range(cores)
        ]
        return jnp.concatenate([h.reshape(block.shape[:-1] + (half,)) for h in halves], axis=-1)

    own_gain = of_features(gain)

    flat = acts[:, 0].reshape(toks, width)
    blocks = local(
        functools.partial(split_kernel, (far, group, cores, rows)),
        [shape((group, toks, cores * half + kvw), bf16)],
        spots,
        flat,
        value_grads[:, 0].reshape(toks, kvw),
    )[0]
    weights_old, blocks = together(master[0].astype(bf16), blocks)
    mine = exchange(blocks, "x").reshape(all_toks, cores * half + kvw)
    weights_old = lax.all_gather(weights_old, "zhi", axis=0, tiled=True)
    mine, weights_old = together(mine, weights_old)

    other = local(
        functools.partial(other_kernel, half),
        [shape((half, kvw), bf16)],
        spots,
        mine,
        own_gain[half:, None],
    )[0]
    partial = local(
        functools.partial(own_kernel, half),
        [shape((half, kvw), bf16)],
        spots,
        mine,
        own_gain[:half, None],
        swap_cores(other),
    )[0]
    grad = lax.psum_scatter(partial, "zhi", scatter_dimension=0, tiled=True)
    weights_other = swap_cores(weights_old)

    mixed, sums = local(
        functools.partial(upstream_kernel, half),
        [shape((all_toks, cores * half), f32), shape((group, 8, all_toks), f32)],
        spots,
        mine,
        weights_old,
        weights_other,
        own_gain[None],
        after=[partial],
    )
    sums = exchange(sums, "x")
    parts = local(
        functools.partial(branch_kernel, (far, rows, width)),
        [shape((layers_y, all_toks, cores * rows), bf16)],
        spots,
        mine,
        mixed,
        sums,
    )[0]
    next_flat, parts = together(next_acts[:, 0].reshape(toks, width), parts)
    came = exchange(parts, "y")

    fresh_blocks = local(
        functools.partial(fresh_kernel, (far, group, cores, rows), reward_ids.shape),
        [shape((toks, cores * half), bf16)] * group,
        spots,
        next_flat,
        norm_gain,
        reward_table,
        scratch=[pltpu.VMEM((toks, width), bf16)],
    )
    fresh_normed = shift(fresh_blocks, "x")

    top_shape = shape((all_toks, cores * rows), bf16)
    top = local(top_kernel, [top_shape], spots, came, after=fresh_normed[1:3])[0]
    behind = [from_behind(top, "zlo", 1)]
    pair = local(pair_kernel, [top_shape], spots, top, behind[0])[0]
    behind.append(from_behind(pair, "zlo", 2))

    near = ("y", "x", "core")
    along = ("zlo", "zhi")
    tile = (8, 128)
    squares = local(
        squares_kernel, [shape((lax.axis_size(near),) + tile, f32)], spots, grad, after=[top]
    )[0]
    squares = exchange(squares, near)
    squares = local(relay_kernel, [shape((lax.axis_size(along),) + tile, f32)], spots, squares, after=fresh_normed)[0]
    squares = exchange(squares, along)
    shard = shape((rows, kvw), f32)
    moment1_new, moment2_new, weights_new = local(
        functools.partial(adam_kernel, lax.axis_size(section) * width * kvw),
        [shard, shard, shape((rows, kvw), bf16)],
        spots,
        squares,
        grad,
        master[0],
        moment1[0],
        moment2[0],
    )
    suffix = local(
        functools.partial(suffix_kernel, group),
        [shape((layers_y * group, toks, cores * rows), bf16)],
        spots,
        came,
        *behind,
    )[0]
    weights_new, suffix = together(weights_new, suffix)
    weights_new = lax.all_gather(weights_new, "zhi", axis=0, tiled=True)
    back = exchange(suffix, ("y", "x"))

    fresh = local(
        functools.partial(values_kernel, half),
        [shape((group, toks, kvw), bf16)],
        spots,
        *fresh_normed,
        weights_new,
        swap_cores(weights_new),
    )[0]
    fresh, back = together(fresh, back)
    fresh = jnp.sum(exchange(fresh, "x").astype(f32), axis=0).astype(bf16)
    fresh_values = fresh.reshape(micro, 1, tok_dev, kvw)

    input_grads = local(
        functools.partial(join_kernel, rows), [shape((toks, width), bf16)], spots, back
    )[0].reshape(micro, 1, tok_dev, width)
    return (input_grads, moment1_new[None], moment2_new[None], fresh_values)


def solution(mesh):
    fine = Mesh(mesh.devices.reshape(factors["section"] + factors["dp"]), axes)
    return jax.shard_map(
        per_device,
        mesh=fine,
        in_specs=(
            P(None, section, dp, None),
            P(section, None),
            P(None, section, dp, None),
            P(section, dp, None),
            P(section, dp, None),
            P(section, dp, None),
            P(None, section, dp, None),
            P(),
            P(),
        ),
        out_specs=(
            P(None, section, dp, None),
            P(section, dp, None),
            P(section, dp, None),
            P(None, section, dp, None),
        ),
        check_vma=False,
    )
```

```python
import functools

import jax
import jax.numpy as jnp
from jax import lax
from jax.experimental import pallas as pl
from jax.experimental.pallas import tpu as pltpu
from jax.sharding import Mesh
from jax.sharding import PartitionSpec as P

rms_epsilon = 1e-05
clip_level = 1.0
beta_first = 0.9
beta_second = 0.95
learn_rate = 0.001
decay_rate = 0.01
adam_epsilon = 1e-08
bias_first = 1.0 - 0.9**10
bias_second = 1.0 - 0.95**10

factors = {"section": (4, 4), "dp": (4, 4, 2)}
axes = ("zlo", "y", "zhi", "x", "core")
section = ("zlo", "y")
dp = ("zhi", "x", "core")
heavy = 2 * 10**10
f32 = jnp.float32
bf16 = jnp.bfloat16


def exchange(blocks, axis):
    return lax.all_to_all(blocks, axis, 0, 0)


def shifts(size):
    return sorted(range(1, size), key=lambda k: -min(k, size - k))


def shift(parts, axis):
    size = len(parts)
    came = [parts[0]] + [None] * (size - 1)
    for k in shifts(size):
        came[k] = lax.ppermute(parts[k], axis, [(i, (i + k) % size) for i in range(size)])
    return came


def swap_cores(block):
    return lax.ppermute(block, "core", [(0, 1), (1, 0)])


def from_behind(block, axis, distance):
    size = lax.axis_size(axis)
    return lax.ppermute(block, axis, [(i + distance, i) for i in range(size - distance)])


def together(*values):
    return lax.optimization_barrier(values)


def inverse_rms(floats):
    return lax.rsqrt(jnp.mean(floats * floats, axis=-1, keepdims=True) + rms_epsilon)


def local(kernel, out_shapes, spots, *arrays, weight=0, scratch=(), after=()):
    def body(spots, *refs):
        kernel(spots, *refs[: len(arrays)], *refs[len(arrays) + len(after) :])

    return pl.pallas_call(
        body,
        out_shape=out_shapes,
        in_specs=[pl.BlockSpec(memory_space=pltpu.SMEM)]
        + [
            pl.BlockSpec(memory_space=pltpu.SMEM if a.dtype == jnp.int32 else pltpu.VMEM)
            for a in arrays
        ]
        + [pl.BlockSpec(memory_space=pl.ANY)] * len(after),
        out_specs=[pl.BlockSpec(memory_space=pltpu.VMEM)] * len(out_shapes),
        scratch_shapes=scratch,
        compiler_params=pltpu.CompilerParams(vmem_limit_bytes=48 * 1024 * 1024),
        cost_estimate=pl.CostEstimate(flops=weight, bytes_accessed=0, transcendentals=0),
    )(spots, *arrays, *after)


def strip_at(start, rows):
    return pl.ds(pl.multiple_of(start, rows), rows)


def split_kernel(sizes, spots, acts, values, master, out, weights):
    far, group, cores, rows = sizes
    core = spots[0]
    half = far * rows
    weights[...] = master[...].astype(bf16)
    floats = acts[...].astype(f32)
    scaled = (values[...].astype(f32) * inverse_rms(floats)).astype(bf16)
    for x in range(group):
        for z in range(far):
            for c in range(cores):
                start = ((z * group + x) * cores + ((core + c) & (cores - 1))) * rows
                out[x, :, c * half + z * rows : c * half + (z + 1) * rows] = acts[
                    :, strip_at(start, rows)
                ]
        out[x, :, cores * half :] = scaled


def split(sizes, spots, acts, values, master):
    far, group, cores, rows = sizes
    toks, width = acts.shape
    kvw = values.shape[1]
    steps = 4
    cut = toks // steps
    lanes = cores * far * rows + kvw
    return pl.pallas_call(
        functools.partial(split_kernel, sizes),
        grid=(steps,),
        out_shape=[
            jax.ShapeDtypeStruct((group, toks, lanes), bf16),
            jax.ShapeDtypeStruct((rows, kvw), bf16),
        ],
        in_specs=[
            pl.BlockSpec(memory_space=pltpu.SMEM),
            pl.BlockSpec((cut, width), lambda i: (i, 0)),
            pl.BlockSpec((cut, kvw), lambda i: (i, 0)),
            pl.BlockSpec((rows // steps, kvw), lambda i: (i, 0)),
        ],
        out_specs=[
            pl.BlockSpec((group, cut, lanes), lambda i: (0, i, 0)),
            pl.BlockSpec((rows // steps, kvw), lambda i: (i, 0)),
        ],
        compiler_params=pltpu.CompilerParams(vmem_limit_bytes=63 * 1024 * 1024),
        cost_estimate=pl.CostEstimate(flops=0, bytes_accessed=0, transcendentals=0),
    )(spots, acts, values, master)


def other_kernel(half, spots, mine, gain, out):
    left = mine[:, half : 2 * half]
    part = lax.dot_general(
        left, mine[:, 2 * half :], (((0,), (0,)), ((), ())), preferred_element_type=f32
    )
    out[...] = (part * gain[...]).astype(bf16)


def own_kernel(half, spots, mine, gain, out):
    part = lax.dot_general(
        mine[:, :half], mine[:, 2 * half :], (((0,), (0,)), ((), ())), preferred_element_type=f32
    )
    out[...] = part * gain[...]


def add_kernel(spots, own, came, out):
    out[...] = (own[...] + came[...].astype(f32)).astype(bf16)


def upstream_kernel(half, spots, mine, own, other, gain, mixed, sums):
    values = mine[:, 2 * half :]
    squares, products = 0.0, 0.0
    for c, weights in enumerate((own, other)):
        cols = slice(c * half, (c + 1) * half)
        part = lax.dot_general(
            values, weights[...], (((1,), (1,)), ((), ())), preferred_element_type=f32
        )
        part = part * gain[:, cols]
        mixed[:, cols] = part
        floats = mine[:, cols].astype(f32)
        squares = squares + jnp.sum(floats * floats, axis=1, keepdims=True)
        products = products + jnp.sum(floats * part, axis=1, keepdims=True)
    lane = lax.broadcasted_iota(jnp.int32, (mine.shape[0], 128), 1)
    both = jnp.where(lane == 0, squares, jnp.where(lane == 1, products, 0.0))
    for x in range(sums.shape[0]):
        sums[x] = both.T[:8]


def branch_kernel(sizes, spots, mine, mixed, sums, out):
    far, rows, width = sizes
    half = far * rows
    both = jnp.concatenate([jnp.sum(sums[...], axis=0)] * 16, axis=0).T
    inv = lax.rsqrt(both[:, 0:1] / width + rms_epsilon)
    pull = inv * (inv * (both[:, 1:2] / width))
    for z in range(far):
        for c in range(mixed.shape[1] // half):
            cols = slice(c * half + z * rows, c * half + (z + 1) * rows)
            block = mixed[:, cols] - mine[:, cols].astype(f32) * pull
            out[z, :, c * rows : (c + 1) * rows] = block.astype(bf16)


def fresh_kernel(sizes, spots, ids, acts, gain, table, *refs):
    *outs, normed = refs
    far, group, cores, rows = sizes
    micro = ids.shape[0]
    half = far * rows
    floats = acts[...].astype(f32)
    toks = floats.shape[0]
    row = lax.broadcasted_iota(jnp.int32, (toks, 1), 0)
    for m in range(micro):
        bin_id = ids[m, spots[3]]
        embed = jnp.zeros((1, floats.shape[1]), f32)
        for b in range(table.shape[0]):
            embed = jnp.where(bin_id == b, table[b : b + 1, :].astype(f32), embed)
        first = jnp.logical_and(row == m * (toks // micro), spots[2] == 0)
        floats = jnp.where(first, embed, floats)
    normed[...] = (floats * inverse_rms(floats) * gain[...]).astype(bf16)
    for k, out in enumerate(outs):
        x = (spots[4] + k) & (group - 1)
        for z in range(far):
            for c in range(cores):
                start = ((z * group + x) * cores + ((spots[0] + c) & (cores - 1))) * rows
                out[:, c * half + z * rows : c * half + (z + 1) * rows] = normed[
                    :, strip_at(start, rows)
                ]


def first_kernel(half, spots, *refs):
    *blocks, weights, out = refs
    for k, block in enumerate(blocks):
        part = jnp.dot(block[:, :half], weights[...], preferred_element_type=f32)
        out[(spots[4] - k) & (len(blocks) - 1)] = part


def second_kernel(half, spots, *refs):
    *blocks, weights, first, out = refs
    for k, block in enumerate(blocks):
        x = (spots[4] - k) & (len(blocks) - 1)
        part = jnp.dot(block[:, half:], weights[...], preferred_element_type=f32)
        out[x] = (first[x] + part).astype(bf16)


def top_kernel(spots, came, out):
    out[...] = jnp.sum(came[...].astype(f32), axis=0).astype(bf16)


def suffix_kernel(group, spots, came, *refs):
    *parts, out = refs
    block = sum(part[...].astype(f32) for part in parts)
    toks = out.shape[1]
    for layer in reversed(range(came.shape[0])):
        block = block + came[layer].astype(f32)
        for x in range(group):
            out[layer * group + x] = block[x * toks : (x + 1) * toks].astype(bf16)


def squares_kernel(spots, grad, out):
    floats = grad[...].astype(f32)
    out[...] = jnp.broadcast_to(jnp.sum(floats * floats), out.shape)


def relay_kernel(spots, sums, out):
    out[...] = jnp.broadcast_to(jnp.sum(sums[...], axis=0, keepdims=True), out.shape)


def adam_kernel(entries, spots, sums, grad, master, first, second, first_new, second_new, weights):
    squares = jnp.sum(sums[...], axis=0)
    clip = jnp.minimum(1.0, clip_level / jnp.sqrt(squares / entries + 1e-12))[0:1, 0:1]
    clipped = grad[...].astype(f32) * clip
    moment1 = beta_first * first[...] + (1.0 - beta_first) * clipped
    moment2 = beta_second * second[...] + (1.0 - beta_second) * clipped * clipped
    first_new[...] = moment1
    second_new[...] = moment2
    update = (
        moment1 / bias_first / (jnp.sqrt(moment2 / bias_second) + adam_epsilon)
        + decay_rate * master[...]
    )
    weights[...] = (master[...] - learn_rate * update).astype(bf16)


def join_kernel(rows, spots, back, out):
    cores = back.shape[2] // rows
    for j in range(back.shape[0]):
        for c in range(cores):
            start = (j * cores + ((spots[0] + c) & (cores - 1))) * rows
            out[:, strip_at(start, rows)] = back[j, :, c * rows : (c + 1) * rows]


def per_device(
    acts, norm_gain, value_grads, master, moment1, moment2, next_acts, reward_table, reward_ids
):
    micro, _, tok_dev, width = acts.shape
    kvw = value_grads.shape[3]
    toks = micro * tok_dev
    far = lax.axis_size("zhi")
    group = lax.axis_size("x")
    cores = lax.axis_size("core")
    layers_y = lax.axis_size("y")
    rows = width // (far * group * cores)
    half = far * rows
    all_toks = group * toks
    core, spot_y, spot_x = (lax.axis_index(name) for name in ("core", "y", "x"))
    spots = jnp.stack([core, spot_y, lax.axis_index(section), lax.axis_index(dp), spot_x])
    shape = jax.ShapeDtypeStruct
    gain = norm_gain[0]

    def of_features(block):
        split = block.reshape(block.shape[:-1] + (far, group, cores, rows))
        split = lax.dynamic_index_in_dim(split, spot_x, split.ndim - 3, False)
        halves = [
            lax.dynamic_index_in_dim(split, core ^ c, split.ndim - 2, False) for c in range(cores)
        ]
        return jnp.concatenate([h.reshape(block.shape[:-1] + (half,)) for h in halves], axis=-1)

    own_gain = of_features(gain)

    flat = acts[:, 0].reshape(toks, width)
    blocks, weights_old = split(
        (far, group, cores, rows), spots, flat, value_grads[:, 0].reshape(toks, kvw), master[0]
    )
    mine = exchange(blocks, "x").reshape(all_toks, cores * half + kvw)
    weights_old = lax.all_gather(weights_old, "zhi", axis=0, tiled=True)
    mine, weights_old = together(mine, weights_old)

    other = local(
        functools.partial(other_kernel, half),
        [shape((half, kvw), bf16)],
        spots,
        mine,
        own_gain[half:, None],
    )[0]
    came = swap_cores(other)
    own = local(
        functools.partial(own_kernel, half),
        [shape((half, kvw), f32)],
        spots,
        mine,
        own_gain[:half, None],
        after=[other],
    )[0]
    partial = local(add_kernel, [shape((half, kvw), bf16)], spots, own, came)[0]
    partial, weights_old = together(partial, weights_old)
    grad = lax.psum_scatter(partial, "zhi", scatter_dimension=0, tiled=True)
    weights_other = swap_cores(weights_old)

    mixed, sums = local(
        functools.partial(upstream_kernel, half),
        [shape((all_toks, cores * half), f32), shape((group, 8, all_toks), f32)],
        spots,
        mine,
        weights_old,
        weights_other,
        own_gain[None],
        after=[partial],
    )
    sums = exchange(sums, "x")
    parts = local(
        functools.partial(branch_kernel, (far, rows, width)),
        [shape((layers_y, all_toks, cores * rows), bf16)],
        spots,
        mine,
        mixed,
        sums,
    )[0]
    next_flat, parts = together(next_acts[:, 0].reshape(toks, width), parts)
    came = exchange(parts, "y")

    fresh_blocks = local(
        functools.partial(fresh_kernel, (far, group, cores, rows)),
        [shape((toks, cores * half), bf16)] * group,
        spots,
        reward_ids,
        next_flat,
        norm_gain,
        reward_table,
        scratch=[pltpu.VMEM((toks, width), bf16)],
    )
    fresh_normed = shift(fresh_blocks, "x")

    top_shape = shape((all_toks, cores * rows), bf16)
    top = local(top_kernel, [top_shape], spots, came, after=fresh_normed[1:3])[0]
    sections = lax.axis_size("zlo")
    behind = [from_behind(top, "zlo", k) for k in range(sections - 1, 0, -1)]

    near = ("y", "x", "core")
    along = ("zlo", "zhi")
    tile = (8, 128)
    squares = local(
        squares_kernel, [shape((lax.axis_size(near),) + tile, f32)], spots, grad, after=[top]
    )[0]
    squares = exchange(squares, near)
    squares = local(relay_kernel, [shape((lax.axis_size(along),) + tile, f32)], spots, squares, after=fresh_normed + behind)[0]
    squares = exchange(squares, along)
    shard = shape((rows, kvw), f32)
    moment1_new, moment2_new, weights_new = local(
        functools.partial(adam_kernel, lax.axis_size(section) * width * kvw),
        [shard, shard, shape((rows, kvw), bf16)],
        spots,
        squares,
        grad,
        master[0],
        moment1[0],
        moment2[0],
    )
    suffix = local(
        functools.partial(suffix_kernel, group),
        [shape((layers_y * group, toks, cores * rows), bf16)],
        spots,
        came,
        *behind,
    )[0]
    weights_new, suffix = together(weights_new, suffix)
    weights_new = lax.all_gather(weights_new, "zhi", axis=0, tiled=True)
    back = exchange(suffix, ("y", "x"))

    weights_other = swap_cores(weights_new)
    first = local(
        functools.partial(first_kernel, half),
        [shape((group, toks, kvw), f32)],
        spots,
        *fresh_normed,
        weights_new,
    )[0]
    fresh = local(
        functools.partial(second_kernel, half),
        [shape((group, toks, kvw), bf16)],
        spots,
        *fresh_normed,
        weights_other,
        first,
    )[0]
    fresh, back = together(fresh, back)
    fresh = jnp.sum(exchange(fresh, "x").astype(f32), axis=0).astype(bf16)
    fresh_values = fresh.reshape(micro, 1, tok_dev, kvw)

    input_grads = local(
        functools.partial(join_kernel, rows), [shape((toks, width), bf16)], spots, back
    )[0].reshape(micro, 1, tok_dev, width)
    return (input_grads, moment1_new[None], moment2_new[None], fresh_values)


def solution(mesh):
    fine = Mesh(mesh.devices.reshape(factors["section"] + factors["dp"]), axes)
    return jax.shard_map(
        per_device,
        mesh=fine,
        in_specs=(
            P(None, section, dp, None),
            P(section, None),
            P(None, section, dp, None),
            P(section, dp, None),
            P(section, dp, None),
            P(section, dp, None),
            P(None, section, dp, None),
            P(),
            P(),
        ),
        out_specs=(
            P(None, section, dp, None),
            P(section, dp, None),
            P(section, dp, None),
            P(None, section, dp, None),
        ),
        check_vma=False,
    )
```

```python
import functools

import jax
import jax.numpy as jnp
from jax import lax
from jax.experimental import pallas as pl
from jax.experimental.pallas import tpu as pltpu
from jax.sharding import Mesh
from jax.sharding import PartitionSpec as P

rms_epsilon = 1e-05
clip_level = 1.0
beta_first = 0.9
beta_second = 0.95
learn_rate = 0.001
decay_rate = 0.01
adam_epsilon = 1e-08
bias_first = 1.0 - 0.9**10
bias_second = 1.0 - 0.95**10

factors = {"section": (4, 4), "dp": (4, 4, 2)}
axes = ("zlo", "y", "zhi", "x", "core")
section = ("zlo", "y")
dp = ("zhi", "x", "core")
heavy = 2 * 10**10
f32 = jnp.float32
bf16 = jnp.bfloat16


def exchange(blocks, axis):
    return lax.all_to_all(blocks, axis, 0, 0)


def shifts(size):
    return sorted(range(1, size), key=lambda k: -min(k, size - k))


def shift(parts, axis):
    size = len(parts)
    came = [parts[0]] + [None] * (size - 1)
    for k in shifts(size):
        came[k] = lax.ppermute(parts[k], axis, [(i, (i + k) % size) for i in range(size)])
    return came


def swap_cores(block):
    return lax.ppermute(block, "core", [(0, 1), (1, 0)])


def from_behind(block, axis, distance):
    size = lax.axis_size(axis)
    return lax.ppermute(block, axis, [(i + distance, i) for i in range(size - distance)])


def together(*values):
    return lax.optimization_barrier(values)


def inverse_rms(floats):
    return lax.rsqrt(jnp.mean(floats * floats, axis=-1, keepdims=True) + rms_epsilon)


def local(kernel, out_shapes, spots, *arrays, weight=0, scratch=(), after=()):
    def body(spots, *refs):
        kernel(spots, *refs[: len(arrays)], *refs[len(arrays) + len(after) :])

    return pl.pallas_call(
        body,
        out_shape=out_shapes,
        in_specs=[pl.BlockSpec(memory_space=pltpu.SMEM)]
        + [
            pl.BlockSpec(memory_space=pltpu.SMEM if a.dtype == jnp.int32 else pltpu.VMEM)
            for a in arrays
        ]
        + [pl.BlockSpec(memory_space=pl.ANY)] * len(after),
        out_specs=[pl.BlockSpec(memory_space=pltpu.VMEM)] * len(out_shapes),
        scratch_shapes=scratch,
        compiler_params=pltpu.CompilerParams(vmem_limit_bytes=48 * 1024 * 1024),
        cost_estimate=pl.CostEstimate(flops=weight, bytes_accessed=0, transcendentals=0),
    )(spots, *arrays, *after)


def strip_at(start, rows):
    return pl.ds(pl.multiple_of(start, rows), rows)


def split_kernel(sizes, spots, acts, values, master, out, weights):
    far, group, cores, rows = sizes
    core = spots[0]
    half = far * rows
    weights[...] = master[...].astype(bf16)
    floats = acts[...].astype(f32)
    scaled = (values[...].astype(f32) * inverse_rms(floats)).astype(bf16)
    for x in range(group):
        for z in range(far):
            for c in range(cores):
                start = ((z * group + x) * cores + ((core + c) & (cores - 1))) * rows
                out[x, :, c * half + z * rows : c * half + (z + 1) * rows] = acts[
                    :, strip_at(start, rows)
                ]
        out[x, :, cores * half :] = scaled


def split(sizes, spots, acts, values, master):
    far, group, cores, rows = sizes
    toks, width = acts.shape
    kvw = values.shape[1]
    steps = 4
    cut = toks // steps
    lanes = cores * far * rows + kvw
    return pl.pallas_call(
        functools.partial(split_kernel, sizes),
        grid=(steps,),
        out_shape=[
            jax.ShapeDtypeStruct((group, toks, lanes), bf16),
            jax.ShapeDtypeStruct((rows, kvw), bf16),
        ],
        in_specs=[
            pl.BlockSpec(memory_space=pltpu.SMEM),
            pl.BlockSpec((cut, width), lambda i: (i, 0)),
            pl.BlockSpec((cut, kvw), lambda i: (i, 0)),
            pl.BlockSpec((rows // steps, kvw), lambda i: (i, 0)),
        ],
        out_specs=[
            pl.BlockSpec((group, cut, lanes), lambda i: (0, i, 0)),
            pl.BlockSpec((rows // steps, kvw), lambda i: (i, 0)),
        ],
        compiler_params=pltpu.CompilerParams(vmem_limit_bytes=63 * 1024 * 1024),
        cost_estimate=pl.CostEstimate(flops=0, bytes_accessed=0, transcendentals=0),
    )(spots, acts, values, master)


def other_kernel(half, spots, mine, gain, out):
    left = mine[:, half : 2 * half]
    part = lax.dot_general(
        left, mine[:, 2 * half :], (((0,), (0,)), ((), ())), preferred_element_type=f32
    )
    out[...] = (part * gain[...]).astype(bf16)


def own_kernel(half, spots, mine, gain, out):
    part = lax.dot_general(
        mine[:, :half], mine[:, 2 * half :], (((0,), (0,)), ((), ())), preferred_element_type=f32
    )
    out[...] = part * gain[...]


def add_kernel(spots, own, came, out):
    out[...] = (own[...] + came[...].astype(f32)).astype(bf16)


def upstream_kernel(half, spots, mine, own, other, gain, mixed, sums):
    values = mine[:, 2 * half :]
    squares, products = 0.0, 0.0
    for c, weights in enumerate((own, other)):
        cols = slice(c * half, (c + 1) * half)
        part = lax.dot_general(
            values, weights[...], (((1,), (1,)), ((), ())), preferred_element_type=f32
        )
        part = part * gain[:, cols]
        mixed[:, cols] = part
        floats = mine[:, cols].astype(f32)
        squares = squares + jnp.sum(floats * floats, axis=1, keepdims=True)
        products = products + jnp.sum(floats * part, axis=1, keepdims=True)
    lane = lax.broadcasted_iota(jnp.int32, (mine.shape[0], 128), 1)
    both = jnp.where(lane == 0, squares, jnp.where(lane == 1, products, 0.0))
    for x in range(sums.shape[0]):
        sums[x] = both.T[:8]


def branch_kernel(sizes, spots, mine, mixed, sums, out):
    far, rows, width = sizes
    half = far * rows
    both = jnp.concatenate([jnp.sum(sums[...], axis=0)] * 16, axis=0).T
    inv = lax.rsqrt(both[:, 0:1] / width + rms_epsilon)
    pull = inv * (inv * (both[:, 1:2] / width))
    for z in range(far):
        for c in range(mixed.shape[1] // half):
            cols = slice(c * half + z * rows, c * half + (z + 1) * rows)
            block = mixed[:, cols] - mine[:, cols].astype(f32) * pull
            out[z, :, c * rows : (c + 1) * rows] = block.astype(bf16)


def fresh_kernel(sizes, spots, ids, acts, gain, table, *refs):
    *outs, normed = refs
    far, group, cores, rows = sizes
    micro = ids.shape[0]
    half = far * rows
    floats = acts[...].astype(f32)
    toks = floats.shape[0]
    row = lax.broadcasted_iota(jnp.int32, (toks, 1), 0)
    for m in range(micro):
        bin_id = ids[m, spots[3]]
        embed = jnp.zeros((1, floats.shape[1]), f32)
        for b in range(table.shape[0]):
            embed = jnp.where(bin_id == b, table[b : b + 1, :].astype(f32), embed)
        first = jnp.logical_and(row == m * (toks // micro), spots[2] == 0)
        floats = jnp.where(first, embed, floats)
    normed[...] = (floats * inverse_rms(floats) * gain[...]).astype(bf16)
    for k, out in enumerate(outs):
        x = (spots[4] + k) & (group - 1)
        for z in range(far):
            for c in range(cores):
                start = ((z * group + x) * cores + ((spots[0] + c) & (cores - 1))) * rows
                out[:, c * half + z * rows : c * half + (z + 1) * rows] = normed[
                    :, strip_at(start, rows)
                ]


def first_kernel(half, spots, *refs):
    *blocks, weights, out = refs
    for k, block in enumerate(blocks):
        part = jnp.dot(block[:, :half], weights[...], preferred_element_type=f32)
        out[(spots[4] - k) & (len(blocks) - 1)] = part


def second_kernel(half, spots, *refs):
    *blocks, weights, first, out = refs
    for k, block in enumerate(blocks):
        x = (spots[4] - k) & (len(blocks) - 1)
        part = jnp.dot(block[:, half:], weights[...], preferred_element_type=f32)
        out[x] = (first[x] + part).astype(bf16)


def top_kernel(spots, came, out):
    out[...] = jnp.sum(came[...].astype(f32), axis=0).astype(bf16)


def pair_kernel(spots, top, behind, out):
    out[...] = (top[...].astype(f32) + behind[...].astype(f32)).astype(bf16)


def suffix_kernel(group, spots, came, *refs):
    *parts, out = refs
    block = sum(part[...].astype(f32) for part in parts)
    toks = out.shape[1]
    for layer in reversed(range(came.shape[0])):
        block = block + came[layer].astype(f32)
        for x in range(group):
            out[layer * group + x] = block[x * toks : (x + 1) * toks].astype(bf16)


def squares_kernel(spots, grad, out):
    floats = grad[...].astype(f32)
    out[...] = jnp.broadcast_to(jnp.sum(floats * floats), out.shape)


def relay_kernel(spots, sums, out):
    out[...] = jnp.broadcast_to(jnp.sum(sums[...], axis=0, keepdims=True), out.shape)


def adam_kernel(entries, spots, sums, grad, master, first, second, first_new, second_new, weights):
    squares = jnp.sum(sums[...], axis=0)
    clip = jnp.minimum(1.0, clip_level / jnp.sqrt(squares / entries + 1e-12))[0:1, 0:1]
    clipped = grad[...].astype(f32) * clip
    moment1 = beta_first * first[...] + (1.0 - beta_first) * clipped
    moment2 = beta_second * second[...] + (1.0 - beta_second) * clipped * clipped
    first_new[...] = moment1
    second_new[...] = moment2
    update = (
        moment1 / bias_first / (jnp.sqrt(moment2 / bias_second) + adam_epsilon)
        + decay_rate * master[...]
    )
    weights[...] = (master[...] - learn_rate * update).astype(bf16)


def join_kernel(rows, spots, back, out):
    cores = back.shape[2] // rows
    for j in range(back.shape[0]):
        for c in range(cores):
            start = (j * cores + ((spots[0] + c) & (cores - 1))) * rows
            out[:, strip_at(start, rows)] = back[j, :, c * rows : (c + 1) * rows]


def per_device(
    acts, norm_gain, value_grads, master, moment1, moment2, next_acts, reward_table, reward_ids
):
    micro, _, tok_dev, width = acts.shape
    kvw = value_grads.shape[3]
    toks = micro * tok_dev
    far = lax.axis_size("zhi")
    group = lax.axis_size("x")
    cores = lax.axis_size("core")
    layers_y = lax.axis_size("y")
    rows = width // (far * group * cores)
    half = far * rows
    all_toks = group * toks
    core, spot_y, spot_x = (lax.axis_index(name) for name in ("core", "y", "x"))
    spots = jnp.stack([core, spot_y, lax.axis_index(section), lax.axis_index(dp), spot_x])
    shape = jax.ShapeDtypeStruct
    gain = norm_gain[0]

    def of_features(block):
        split = block.reshape(block.shape[:-1] + (far, group, cores, rows))
        split = lax.dynamic_index_in_dim(split, spot_x, split.ndim - 3, False)
        halves = [
            lax.dynamic_index_in_dim(split, core ^ c, split.ndim - 2, False) for c in range(cores)
        ]
        return jnp.concatenate([h.reshape(block.shape[:-1] + (half,)) for h in halves], axis=-1)

    own_gain = of_features(gain)

    flat = acts[:, 0].reshape(toks, width)
    blocks, weights_old = split(
        (far, group, cores, rows), spots, flat, value_grads[:, 0].reshape(toks, kvw), master[0]
    )
    mine = exchange(blocks, "x").reshape(all_toks, cores * half + kvw)
    weights_old = lax.all_gather(weights_old, "zhi", axis=0, tiled=True)
    mine, weights_old = together(mine, weights_old)

    other = local(
        functools.partial(other_kernel, half),
        [shape((half, kvw), bf16)],
        spots,
        mine,
        own_gain[half:, None],
    )[0]
    came = swap_cores(other)
    own = local(
        functools.partial(own_kernel, half),
        [shape((half, kvw), f32)],
        spots,
        mine,
        own_gain[:half, None],
        after=[other],
    )[0]
    partial = local(add_kernel, [shape((half, kvw), bf16)], spots, own, came)[0]
    partial, weights_old = together(partial, weights_old)
    grad = lax.psum_scatter(partial, "zhi", scatter_dimension=0, tiled=True)
    weights_other = swap_cores(weights_old)

    mixed, sums = local(
        functools.partial(upstream_kernel, half),
        [shape((all_toks, cores * half), f32), shape((group, 8, all_toks), f32)],
        spots,
        mine,
        weights_old,
        weights_other,
        own_gain[None],
        after=[partial],
    )
    sums = exchange(sums, "x")
    parts = local(
        functools.partial(branch_kernel, (far, rows, width)),
        [shape((layers_y, all_toks, cores * rows), bf16)],
        spots,
        mine,
        mixed,
        sums,
    )[0]
    next_flat, parts = together(next_acts[:, 0].reshape(toks, width), parts)
    came = exchange(parts, "y")

    fresh_blocks = local(
        functools.partial(fresh_kernel, (far, group, cores, rows)),
        [shape((toks, cores * half), bf16)] * group,
        spots,
        reward_ids,
        next_flat,
        norm_gain,
        reward_table,
        scratch=[pltpu.VMEM((toks, width), bf16)],
    )
    fresh_normed = shift(fresh_blocks, "x")

    top_shape = shape((all_toks, cores * rows), bf16)
    top = local(top_kernel, [top_shape], spots, came, after=fresh_normed[1:3])[0]
    behind = [from_behind(top, "zlo", 1)]
    pair = local(pair_kernel, [top_shape], spots, top, behind[0])[0]
    behind.append(from_behind(pair, "zlo", 2))

    near = ("y", "x", "core")
    along = ("zlo", "zhi")
    tile = (8, 128)
    squares = local(
        squares_kernel, [shape((lax.axis_size(near),) + tile, f32)], spots, grad, after=[top]
    )[0]
    squares = exchange(squares, near)
    squares = local(relay_kernel, [shape((lax.axis_size(along),) + tile, f32)], spots, squares, after=fresh_normed)[0]
    squares = exchange(squares, along)
    suffix = local(
        functools.partial(suffix_kernel, group),
        [shape((layers_y * group, toks, cores * rows), bf16)],
        spots,
        came,
        *behind,
    )[0]
    shard = shape((rows, kvw), f32)
    moment1_new, moment2_new, weights_new = local(
        functools.partial(adam_kernel, lax.axis_size(section) * width * kvw),
        [shard, shard, shape((rows, kvw), bf16)],
        spots,
        squares,
        grad,
        master[0],
        moment1[0],
        moment2[0],
        after=[suffix],
    )
    weights_new, suffix = together(weights_new, suffix)
    weights_new = lax.all_gather(weights_new, "zhi", axis=0, tiled=True)
    back = exchange(suffix, ("y", "x"))

    weights_other = swap_cores(weights_new)
    first = local(
        functools.partial(first_kernel, half),
        [shape((group, toks, kvw), f32)],
        spots,
        *fresh_normed,
        weights_new,
    )[0]
    fresh = local(
        functools.partial(second_kernel, half),
        [shape((group, toks, kvw), bf16)],
        spots,
        *fresh_normed,
        weights_other,
        first,
    )[0]
    fresh, back = together(fresh, back)
    fresh = jnp.sum(exchange(fresh, "x").astype(f32), axis=0).astype(bf16)
    fresh_values = fresh.reshape(micro, 1, tok_dev, kvw)

    input_grads = local(
        functools.partial(join_kernel, rows), [shape((toks, width), bf16)], spots, back
    )[0].reshape(micro, 1, tok_dev, width)
    return (input_grads, moment1_new[None], moment2_new[None], fresh_values)


def solution(mesh):
    fine = Mesh(mesh.devices.reshape(factors["section"] + factors["dp"]), axes)
    return jax.shard_map(
        per_device,
        mesh=fine,
        in_specs=(
            P(None, section, dp, None),
            P(section, None),
            P(None, section, dp, None),
            P(section, dp, None),
            P(section, dp, None),
            P(section, dp, None),
            P(None, section, dp, None),
            P(),
            P(),
        ),
        out_specs=(
            P(None, section, dp, None),
            P(section, dp, None),
            P(section, dp, None),
            P(None, section, dp, None),
        ),
        check_vma=False,
    )
```

```python
import functools

import jax
import jax.numpy as jnp
from jax import lax
from jax.experimental import pallas as pl
from jax.experimental.pallas import tpu as pltpu
from jax.sharding import Mesh
from jax.sharding import PartitionSpec as P

rms_epsilon = 1e-05
clip_level = 1.0
beta_first = 0.9
beta_second = 0.95
learn_rate = 0.001
decay_rate = 0.01
adam_epsilon = 1e-08
bias_first = 1.0 - 0.9**10
bias_second = 1.0 - 0.95**10

factors = {"section": (4, 4), "dp": (4, 4, 2)}
axes = ("zlo", "y", "zhi", "x", "core")
section = ("zlo", "y")
dp = ("zhi", "x", "core")
heavy = 2 * 10**10
f32 = jnp.float32
bf16 = jnp.bfloat16


def exchange(blocks, axis):
    return lax.all_to_all(blocks, axis, 0, 0)


def shifts(size):
    return sorted(range(1, size), key=lambda k: -min(k, size - k))


def shift(parts, axis):
    size = len(parts)
    came = [parts[0]] + [None] * (size - 1)
    for k in shifts(size):
        came[k] = lax.ppermute(parts[k], axis, [(i, (i + k) % size) for i in range(size)])
    return came


def swap_cores(block):
    return lax.ppermute(block, "core", [(0, 1), (1, 0)])


def from_behind(block, axis, distance):
    size = lax.axis_size(axis)
    return lax.ppermute(block, axis, [(i + distance, i) for i in range(size - distance)])


def together(*values):
    return lax.optimization_barrier(values)


def inverse_rms(floats):
    return lax.rsqrt(jnp.mean(floats * floats, axis=-1, keepdims=True) + rms_epsilon)


def local(kernel, out_shapes, spots, *arrays, weight=0, scratch=(), after=()):
    def body(spots, *refs):
        kernel(spots, *refs[: len(arrays)], *refs[len(arrays) + len(after) :])

    return pl.pallas_call(
        body,
        out_shape=out_shapes,
        in_specs=[pl.BlockSpec(memory_space=pltpu.SMEM)]
        + [
            pl.BlockSpec(memory_space=pltpu.SMEM if a.dtype == jnp.int32 else pltpu.VMEM)
            for a in arrays
        ]
        + [pl.BlockSpec(memory_space=pl.ANY)] * len(after),
        out_specs=[pl.BlockSpec(memory_space=pltpu.VMEM)] * len(out_shapes),
        scratch_shapes=scratch,
        compiler_params=pltpu.CompilerParams(vmem_limit_bytes=48 * 1024 * 1024),
        cost_estimate=pl.CostEstimate(flops=weight, bytes_accessed=0, transcendentals=0),
    )(spots, *arrays, *after)


def strip_at(start, rows):
    return pl.ds(pl.multiple_of(start, rows), rows)


def split_kernel(sizes, spots, acts, values, master, out, weights):
    far, group, cores, rows = sizes
    core = spots[0]
    half = far * rows
    weights[...] = master[...].astype(bf16)
    floats = acts[...].astype(f32)
    scaled = (values[...].astype(f32) * inverse_rms(floats)).astype(bf16)
    for x in range(group):
        for z in range(far):
            for c in range(cores):
                start = ((z * group + x) * cores + ((core + c) & (cores - 1))) * rows
                out[x, :, c * half + z * rows : c * half + (z + 1) * rows] = acts[
                    :, strip_at(start, rows)
                ]
        out[x, :, cores * half :] = scaled


def split(sizes, spots, acts, values, master):
    far, group, cores, rows = sizes
    toks, width = acts.shape
    kvw = values.shape[1]
    steps = 4
    cut = toks // steps
    lanes = cores * far * rows + kvw
    return pl.pallas_call(
        functools.partial(split_kernel, sizes),
        grid=(steps,),
        out_shape=[
            jax.ShapeDtypeStruct((group, toks, lanes), bf16),
            jax.ShapeDtypeStruct((rows, kvw), bf16),
        ],
        in_specs=[
            pl.BlockSpec(memory_space=pltpu.SMEM),
            pl.BlockSpec((cut, width), lambda i: (i, 0)),
            pl.BlockSpec((cut, kvw), lambda i: (i, 0)),
            pl.BlockSpec((rows // steps, kvw), lambda i: (i, 0)),
        ],
        out_specs=[
            pl.BlockSpec((group, cut, lanes), lambda i: (0, i, 0)),
            pl.BlockSpec((rows // steps, kvw), lambda i: (i, 0)),
        ],
        compiler_params=pltpu.CompilerParams(vmem_limit_bytes=63 * 1024 * 1024),
        cost_estimate=pl.CostEstimate(flops=0, bytes_accessed=0, transcendentals=0),
    )(spots, acts, values, master)


def other_kernel(half, spots, mine, gain, out):
    left = mine[:, half : 2 * half]
    part = lax.dot_general(
        left, mine[:, 2 * half :], (((0,), (0,)), ((), ())), preferred_element_type=f32
    )
    out[...] = (part * gain[...]).astype(bf16)


def own_kernel(half, spots, mine, gain, out):
    part = lax.dot_general(
        mine[:, :half], mine[:, 2 * half :], (((0,), (0,)), ((), ())), preferred_element_type=f32
    )
    out[...] = part * gain[...]


def add_kernel(spots, own, came, out):
    out[...] = (own[...] + came[...].astype(f32)).astype(bf16)


def upstream_kernel(half, spots, mine, own, other, gain, mixed, sums):
    values = mine[:, 2 * half :]
    squares, products = 0.0, 0.0
    for c, weights in enumerate((own, other)):
        cols = slice(c * half, (c + 1) * half)
        part = lax.dot_general(
            values, weights[...], (((1,), (1,)), ((), ())), preferred_element_type=f32
        )
        part = part * gain[:, cols]
        mixed[:, cols] = part
        floats = mine[:, cols].astype(f32)
        squares = squares + jnp.sum(floats * floats, axis=1, keepdims=True)
        products = products + jnp.sum(floats * part, axis=1, keepdims=True)
    lane = lax.broadcasted_iota(jnp.int32, (mine.shape[0], 128), 1)
    both = jnp.where(lane == 0, squares, jnp.where(lane == 1, products, 0.0))
    for x in range(sums.shape[0]):
        sums[x] = both.T[:8]


def branch_kernel(sizes, spots, mine, mixed, sums, out):
    far, rows, width = sizes
    half = far * rows
    both = jnp.concatenate([jnp.sum(sums[...], axis=0)] * 16, axis=0).T
    inv = lax.rsqrt(both[:, 0:1] / width + rms_epsilon)
    pull = inv * (inv * (both[:, 1:2] / width))
    for z in range(far):
        for c in range(mixed.shape[1] // half):
            cols = slice(c * half + z * rows, c * half + (z + 1) * rows)
            block = mixed[:, cols] - mine[:, cols].astype(f32) * pull
            out[z, :, c * rows : (c + 1) * rows] = block.astype(bf16)


def fresh_kernel(sizes, spots, ids, acts, gain, table, *refs):
    *outs, normed = refs
    far, group, cores, rows = sizes
    micro = ids.shape[0]
    half = far * rows
    floats = acts[...].astype(f32)
    toks = floats.shape[0]
    row = lax.broadcasted_iota(jnp.int32, (toks, 1), 0)
    for m in range(micro):
        bin_id = ids[m, spots[3]]
        embed = jnp.zeros((1, floats.shape[1]), f32)
        for b in range(table.shape[0]):
            embed = jnp.where(bin_id == b, table[b : b + 1, :].astype(f32), embed)
        first = jnp.logical_and(row == m * (toks // micro), spots[2] == 0)
        floats = jnp.where(first, embed, floats)
    normed[...] = (floats * inverse_rms(floats) * gain[...]).astype(bf16)
    for k, out in enumerate(outs):
        x = (spots[4] + k) & (group - 1)
        for z in range(far):
            for c in range(cores):
                start = ((z * group + x) * cores + ((spots[0] + c) & (cores - 1))) * rows
                out[:, c * half + z * rows : c * half + (z + 1) * rows] = normed[
                    :, strip_at(start, rows)
                ]


def first_kernel(half, spots, *refs):
    *blocks, weights, out = refs
    for k, block in enumerate(blocks):
        part = jnp.dot(block[:, :half], weights[...], preferred_element_type=f32)
        out[(spots[4] - k) & (len(blocks) - 1)] = part


def second_kernel(half, spots, *refs):
    *blocks, weights, first, out = refs
    for k, block in enumerate(blocks):
        x = (spots[4] - k) & (len(blocks) - 1)
        part = jnp.dot(block[:, half:], weights[...], preferred_element_type=f32)
        out[x] = (first[x] + part).astype(bf16)


def top_kernel(spots, came, out):
    out[...] = jnp.sum(came[...].astype(f32), axis=0).astype(bf16)


def pair_kernel(spots, top, behind, out):
    out[...] = (top[...].astype(f32) + behind[...].astype(f32)).astype(bf16)


def suffix_kernel(group, spots, came, *refs):
    *parts, out = refs
    block = sum(part[...].astype(f32) for part in parts)
    toks = out.shape[1]
    for layer in reversed(range(came.shape[0])):
        block = block + came[layer].astype(f32)
        for x in range(group):
            out[layer * group + x] = block[x * toks : (x + 1) * toks].astype(bf16)


def squares_kernel(spots, grad, out):
    floats = grad[...].astype(f32)
    out[...] = jnp.broadcast_to(jnp.sum(floats * floats), out.shape)


def relay_kernel(spots, sums, out):
    out[...] = jnp.broadcast_to(jnp.sum(sums[...], axis=0, keepdims=True), out.shape)


def adam_kernel(entries, spots, sums, grad, master, first, second, first_new, second_new, weights):
    squares = jnp.sum(sums[...], axis=0)
    clip = jnp.minimum(1.0, clip_level / jnp.sqrt(squares / entries + 1e-12))[0:1, 0:1]
    clipped = grad[...].astype(f32) * clip
    moment1 = beta_first * first[...] + (1.0 - beta_first) * clipped
    moment2 = beta_second * second[...] + (1.0 - beta_second) * clipped * clipped
    first_new[...] = moment1
    second_new[...] = moment2
    update = (
        moment1 / bias_first / (jnp.sqrt(moment2 / bias_second) + adam_epsilon)
        + decay_rate * master[...]
    )
    weights[...] = (master[...] - learn_rate * update).astype(bf16)


def join_kernel(rows, spots, back, out):
    cores = back.shape[2] // rows
    for j in range(back.shape[0]):
        for c in range(cores):
            start = (j * cores + ((spots[0] + c) & (cores - 1))) * rows
            out[:, strip_at(start, rows)] = back[j, :, c * rows : (c + 1) * rows]


def per_device(
    acts, norm_gain, value_grads, master, moment1, moment2, next_acts, reward_table, reward_ids
):
    micro, _, tok_dev, width = acts.shape
    kvw = value_grads.shape[3]
    toks = micro * tok_dev
    far = lax.axis_size("zhi")
    group = lax.axis_size("x")
    cores = lax.axis_size("core")
    layers_y = lax.axis_size("y")
    rows = width // (far * group * cores)
    half = far * rows
    all_toks = group * toks
    core, spot_y, spot_x = (lax.axis_index(name) for name in ("core", "y", "x"))
    spots = jnp.stack([core, spot_y, lax.axis_index(section), lax.axis_index(dp), spot_x])
    shape = jax.ShapeDtypeStruct
    gain = norm_gain[0]

    def of_features(block):
        split = block.reshape(block.shape[:-1] + (far, group, cores, rows))
        split = lax.dynamic_index_in_dim(split, spot_x, split.ndim - 3, False)
        halves = [
            lax.dynamic_index_in_dim(split, core ^ c, split.ndim - 2, False) for c in range(cores)
        ]
        return jnp.concatenate([h.reshape(block.shape[:-1] + (half,)) for h in halves], axis=-1)

    own_gain = of_features(gain)

    flat = acts[:, 0].reshape(toks, width)
    blocks, weights_old = split(
        (far, group, cores, rows), spots, flat, value_grads[:, 0].reshape(toks, kvw), master[0]
    )
    mine = exchange(blocks, "x").reshape(all_toks, cores * half + kvw)
    weights_old = lax.all_gather(weights_old, "zhi", axis=0, tiled=True)
    mine, weights_old = together(mine, weights_old)

    other = local(
        functools.partial(other_kernel, half),
        [shape((half, kvw), bf16)],
        spots,
        mine,
        own_gain[half:, None],
    )[0]
    came = swap_cores(other)
    own = local(
        functools.partial(own_kernel, half),
        [shape((half, kvw), f32)],
        spots,
        mine,
        own_gain[:half, None],
        after=[other],
    )[0]
    partial = local(add_kernel, [shape((half, kvw), bf16)], spots, own, came)[0]
    partial, weights_old = together(partial, weights_old)
    grad = lax.psum_scatter(partial, "zhi", scatter_dimension=0, tiled=True)
    weights_other = swap_cores(weights_old)

    mixed, sums = local(
        functools.partial(upstream_kernel, half),
        [shape((all_toks, cores * half), f32), shape((group, 8, all_toks), f32)],
        spots,
        mine,
        weights_old,
        weights_other,
        own_gain[None],
        after=[partial],
    )
    sums = exchange(sums, "x")
    parts = local(
        functools.partial(branch_kernel, (far, rows, width)),
        [shape((layers_y, all_toks, cores * rows), bf16)],
        spots,
        mine,
        mixed,
        sums,
    )[0]
    next_flat, parts = together(next_acts[:, 0].reshape(toks, width), parts)
    came = exchange(parts, "y")

    fresh_blocks = local(
        functools.partial(fresh_kernel, (far, group, cores, rows)),
        [shape((toks, cores * half), bf16)] * group,
        spots,
        reward_ids,
        next_flat,
        norm_gain,
        reward_table,
        scratch=[pltpu.VMEM((toks, width), bf16)],
    )
    fresh_normed = shift(fresh_blocks, "x")

    top_shape = shape((all_toks, cores * rows), bf16)
    top = local(top_kernel, [top_shape], spots, came, after=fresh_blocks[:1])[0]
    behind = [from_behind(top, "zlo", 1)]
    pair = local(pair_kernel, [top_shape], spots, top, behind[0])[0]
    behind.append(from_behind(pair, "zlo", 2))

    near = ("y", "x", "core")
    along = ("zlo", "zhi")
    tile = (8, 128)
    squares = local(
        squares_kernel, [shape((lax.axis_size(near),) + tile, f32)], spots, grad, after=[top] + fresh_normed[1:]
    )[0]
    squares = exchange(squares, near)
    squares = local(relay_kernel, [shape((lax.axis_size(along),) + tile, f32)], spots, squares)[0]
    squares = exchange(squares, along)
    suffix = local(
        functools.partial(suffix_kernel, group),
        [shape((layers_y * group, toks, cores * rows), bf16)],
        spots,
        came,
        *behind,
    )[0]
    shard = shape((rows, kvw), f32)
    moment1_new, moment2_new, weights_new = local(
        functools.partial(adam_kernel, lax.axis_size(section) * width * kvw),
        [shard, shard, shape((rows, kvw), bf16)],
        spots,
        squares,
        grad,
        master[0],
        moment1[0],
        moment2[0],
        after=[suffix],
    )
    weights_new, suffix = together(weights_new, suffix)
    weights_new = lax.all_gather(weights_new, "zhi", axis=0, tiled=True)
    back = exchange(suffix, ("y", "x"))

    weights_other = swap_cores(weights_new)
    first = local(
        functools.partial(first_kernel, half),
        [shape((group, toks, kvw), f32)],
        spots,
        *fresh_normed,
        weights_new,
    )[0]
    fresh = local(
        functools.partial(second_kernel, half),
        [shape((group, toks, kvw), bf16)],
        spots,
        *fresh_normed,
        weights_other,
        first,
    )[0]
    fresh, back = together(fresh, back)
    fresh = jnp.sum(exchange(fresh, "x").astype(f32), axis=0).astype(bf16)
    fresh_values = fresh.reshape(micro, 1, tok_dev, kvw)

    input_grads = local(
        functools.partial(join_kernel, rows), [shape((toks, width), bf16)], spots, back
    )[0].reshape(micro, 1, tok_dev, width)
    return (input_grads, moment1_new[None], moment2_new[None], fresh_values)


def solution(mesh):
    fine = Mesh(mesh.devices.reshape(factors["section"] + factors["dp"]), axes)
    return jax.shard_map(
        per_device,
        mesh=fine,
        in_specs=(
            P(None, section, dp, None),
            P(section, None),
            P(None, section, dp, None),
            P(section, dp, None),
            P(section, dp, None),
            P(section, dp, None),
            P(None, section, dp, None),
            P(),
            P(),
        ),
        out_specs=(
            P(None, section, dp, None),
            P(section, dp, None),
            P(section, dp, None),
            P(None, section, dp, None),
        ),
        check_vma=False,
    )
```

```python
import functools

import jax
import jax.numpy as jnp
from jax import lax
from jax.experimental import pallas as pl
from jax.experimental.pallas import tpu as pltpu
from jax.sharding import Mesh
from jax.sharding import PartitionSpec as P

rms_epsilon = 1e-05
clip_level = 1.0
beta_first = 0.9
beta_second = 0.95
learn_rate = 0.001
decay_rate = 0.01
adam_epsilon = 1e-08
bias_first = 1.0 - 0.9**10
bias_second = 1.0 - 0.95**10

factors = {"section": (4, 4), "dp": (4, 4, 2)}
axes = ("zlo", "y", "zhi", "x", "core")
section = ("zlo", "y")
dp = ("zhi", "x", "core")
near = ("x", "core")
heavy = 2 * 10**10
f32 = jnp.float32
bf16 = jnp.bfloat16


def exchange(blocks, axis):
    return lax.all_to_all(blocks, axis, 0, 0)


def shifts(size):
    return sorted(range(1, size), key=lambda k: -min(k, size - k))


def shift(parts, axis):
    size = len(parts)
    came = [parts[0]] + [None] * (size - 1)
    for k in shifts(size):
        came[k] = lax.ppermute(parts[k], axis, [(i, (i + k) % size) for i in range(size)])
    return came


def swap_cores(block):
    return lax.ppermute(block, "core", [(0, 1), (1, 0)])


def from_behind(block, axis, distance):
    size = lax.axis_size(axis)
    return lax.ppermute(block, axis, [(i + distance, i) for i in range(size - distance)])


def together(*values):
    return lax.optimization_barrier(values)


def inverse_rms(floats):
    return lax.rsqrt(jnp.mean(floats * floats, axis=-1, keepdims=True) + rms_epsilon)


def local(kernel, out_shapes, spots, *arrays, weight=0, scratch=(), after=()):
    def body(spots, *refs):
        kernel(spots, *refs[: len(arrays)], *refs[len(arrays) + len(after) :])

    return pl.pallas_call(
        body,
        out_shape=out_shapes,
        in_specs=[pl.BlockSpec(memory_space=pltpu.SMEM)]
        + [
            pl.BlockSpec(memory_space=pltpu.SMEM if a.dtype == jnp.int32 else pltpu.VMEM)
            for a in arrays
        ]
        + [pl.BlockSpec(memory_space=pl.ANY)] * len(after),
        out_specs=[pl.BlockSpec(memory_space=pltpu.VMEM)] * len(out_shapes),
        scratch_shapes=scratch,
        compiler_params=pltpu.CompilerParams(vmem_limit_bytes=48 * 1024 * 1024),
        cost_estimate=pl.CostEstimate(flops=weight, bytes_accessed=0, transcendentals=0),
    )(spots, *arrays, *after)


def strip_at(start, rows):
    return pl.ds(pl.multiple_of(start, rows), rows)


def split_kernel(sizes, spots, acts, values, master, out, weights):
    far, group, cores, rows = sizes
    core = spots[0]
    half = far * rows
    weights[...] = master[...].astype(bf16)
    floats = acts[...].astype(f32)
    scaled = (values[...].astype(f32) * inverse_rms(floats)).astype(bf16)
    for x in range(group):
        for z in range(far):
            for c in range(cores):
                start = ((z * group + x) * cores + ((core + c) & (cores - 1))) * rows
                out[x, :, c * half + z * rows : c * half + (z + 1) * rows] = acts[
                    :, strip_at(start, rows)
                ]
        out[x, :, cores * half :] = scaled


def split(sizes, spots, acts, values, master):
    far, group, cores, rows = sizes
    toks, width = acts.shape
    kvw = values.shape[1]
    steps = 4
    cut = toks // steps
    lanes = cores * far * rows + kvw
    return pl.pallas_call(
        functools.partial(split_kernel, sizes),
        grid=(steps,),
        out_shape=[
            jax.ShapeDtypeStruct((group, toks, lanes), bf16),
            jax.ShapeDtypeStruct((rows, kvw), bf16),
        ],
        in_specs=[
            pl.BlockSpec(memory_space=pltpu.SMEM),
            pl.BlockSpec((cut, width), lambda i: (i, 0)),
            pl.BlockSpec((cut, kvw), lambda i: (i, 0)),
            pl.BlockSpec((rows // steps, kvw), lambda i: (i, 0)),
        ],
        out_specs=[
            pl.BlockSpec((group, cut, lanes), lambda i: (0, i, 0)),
            pl.BlockSpec((rows // steps, kvw), lambda i: (i, 0)),
        ],
        compiler_params=pltpu.CompilerParams(vmem_limit_bytes=63 * 1024 * 1024),
        cost_estimate=pl.CostEstimate(flops=0, bytes_accessed=0, transcendentals=0),
    )(spots, acts, values, master)


def other_kernel(half, spots, mine, gain, out):
    left = mine[:, half : 2 * half]
    part = lax.dot_general(
        left, mine[:, 2 * half :], (((0,), (0,)), ((), ())), preferred_element_type=f32
    )
    out[...] = (part * gain[...]).astype(bf16)


def own_kernel(half, spots, mine, gain, out):
    part = lax.dot_general(
        mine[:, :half], mine[:, 2 * half :], (((0,), (0,)), ((), ())), preferred_element_type=f32
    )
    out[...] = part * gain[...]


def add_kernel(spots, own, came, out):
    out[...] = (own[...] + came[...].astype(f32)).astype(bf16)


def upstream_kernel(half, spots, mine, own, other, gain, mixed, sums):
    values = mine[:, 2 * half :]
    squares, products = 0.0, 0.0
    for c, weights in enumerate((own, other)):
        cols = slice(c * half, (c + 1) * half)
        part = lax.dot_general(
            values, weights[...], (((1,), (1,)), ((), ())), preferred_element_type=f32
        )
        part = part * gain[:, cols]
        mixed[:, cols] = part
        floats = mine[:, cols].astype(f32)
        squares = squares + jnp.sum(floats * floats, axis=1, keepdims=True)
        products = products + jnp.sum(floats * part, axis=1, keepdims=True)
    lane = lax.broadcasted_iota(jnp.int32, (mine.shape[0], 128), 1)
    both = jnp.where(lane == 0, squares, jnp.where(lane == 1, products, 0.0))
    for x in range(sums.shape[0]):
        sums[x] = both.T[:8]


def branch_kernel(sizes, spots, mine, mixed, sums, out):
    far, rows, width = sizes
    half = far * rows
    both = jnp.concatenate([jnp.sum(sums[...], axis=0)] * 16, axis=0).T
    inv = lax.rsqrt(both[:, 0:1] / width + rms_epsilon)
    pull = inv * (inv * (both[:, 1:2] / width))
    for z in range(far):
        for c in range(mixed.shape[1] // half):
            cols = slice(c * half + z * rows, c * half + (z + 1) * rows)
            block = mixed[:, cols] - mine[:, cols].astype(f32) * pull
            out[z, :, c * rows : (c + 1) * rows] = block.astype(bf16)


def fresh_kernel(sizes, spots, ids, acts, gain, table, *refs):
    *outs, normed = refs
    far, group, cores, rows = sizes
    micro = ids.shape[0]
    half = far * rows
    floats = acts[...].astype(f32)
    toks = floats.shape[0]
    row = lax.broadcasted_iota(jnp.int32, (toks, 1), 0)
    for m in range(micro):
        bin_id = ids[m, spots[3]]
        embed = jnp.zeros((1, floats.shape[1]), f32)
        for b in range(table.shape[0]):
            embed = jnp.where(bin_id == b, table[b : b + 1, :].astype(f32), embed)
        first = jnp.logical_and(row == m * (toks // micro), spots[2] == 0)
        floats = jnp.where(first, embed, floats)
    normed[...] = (floats * inverse_rms(floats) * gain[...]).astype(bf16)
    for k, out in enumerate(outs):
        x = (spots[4] + k) & (group - 1)
        for z in range(far):
            for c in range(cores):
                start = ((z * group + x) * cores + ((spots[0] + c) & (cores - 1))) * rows
                out[:, c * half + z * rows : c * half + (z + 1) * rows] = normed[
                    :, strip_at(start, rows)
                ]


def first_kernel(half, spots, *refs):
    *blocks, weights, out = refs
    for k, block in enumerate(blocks):
        part = jnp.dot(block[:, :half], weights[...], preferred_element_type=f32)
        out[(spots[4] - k) & (len(blocks) - 1)] = part


def second_kernel(half, spots, *refs):
    *blocks, weights, first, out = refs
    for k, block in enumerate(blocks):
        x = (spots[4] - k) & (len(blocks) - 1)
        part = jnp.dot(block[:, half:], weights[...], preferred_element_type=f32)
        out[x] = (first[x] + part).astype(bf16)


def top_kernel(spots, came, out):
    out[...] = jnp.sum(came[...].astype(f32), axis=0).astype(bf16)


def pair_kernel(spots, top, behind, out):
    out[...] = (top[...].astype(f32) + behind[...].astype(f32)).astype(bf16)


def suffix_kernel(group, spots, came, *refs):
    *parts, out = refs
    block = sum(part[...].astype(f32) for part in parts)
    toks = out.shape[1]
    for layer in reversed(range(came.shape[0])):
        block = block + came[layer].astype(f32)
        for x in range(group):
            out[layer * group + x] = block[x * toks : (x + 1) * toks].astype(bf16)


def squares_kernel(spots, grad, out):
    floats = grad[...].astype(f32)
    out[...] = jnp.broadcast_to(jnp.sum(floats * floats), out.shape)


def relay_kernel(spots, sums, out):
    out[...] = jnp.broadcast_to(jnp.sum(sums[...], axis=0, keepdims=True), out.shape)


def adam_kernel(entries, spots, sums, grad, master, first, second, first_new, second_new, weights):
    squares = jnp.sum(sums[...], axis=0)
    clip = jnp.minimum(1.0, clip_level / jnp.sqrt(squares / entries + 1e-12))[0:1, 0:1]
    clipped = grad[...].astype(f32) * clip
    moment1 = beta_first * first[...] + (1.0 - beta_first) * clipped
    moment2 = beta_second * second[...] + (1.0 - beta_second) * clipped * clipped
    first_new[...] = moment1
    second_new[...] = moment2
    update = (
        moment1 / bias_first / (jnp.sqrt(moment2 / bias_second) + adam_epsilon)
        + decay_rate * master[...]
    )
    weights[...] = (master[...] - learn_rate * update).astype(bf16)


def join_kernel(rows, spots, back, out):
    cores = back.shape[2] // rows
    for j in range(back.shape[0]):
        for c in range(cores):
            start = (j * cores + ((spots[0] + c) & (cores - 1))) * rows
            out[:, strip_at(start, rows)] = back[j, :, c * rows : (c + 1) * rows]


def per_device(
    acts, norm_gain, value_grads, master, moment1, moment2, next_acts, reward_table, reward_ids
):
    micro, _, tok_dev, width = acts.shape
    kvw = value_grads.shape[3]
    toks = micro * tok_dev
    far = lax.axis_size("zhi")
    group = lax.axis_size("x")
    cores = lax.axis_size("core")
    layers_y = lax.axis_size("y")
    rows = width // (far * group * cores)
    half = far * rows
    all_toks = group * toks
    core, spot_y, spot_x = (lax.axis_index(name) for name in ("core", "y", "x"))
    spots = jnp.stack([core, spot_y, lax.axis_index(section), lax.axis_index(dp), spot_x])
    shape = jax.ShapeDtypeStruct
    gain = norm_gain[0]

    def of_features(block):
        split = block.reshape(block.shape[:-1] + (far, group, cores, rows))
        split = lax.dynamic_index_in_dim(split, spot_x, split.ndim - 3, False)
        halves = [
            lax.dynamic_index_in_dim(split, core ^ c, split.ndim - 2, False) for c in range(cores)
        ]
        return jnp.concatenate([h.reshape(block.shape[:-1] + (half,)) for h in halves], axis=-1)

    own_gain = of_features(gain)

    flat = acts[:, 0].reshape(toks, width)
    blocks, weights_old = split(
        (far, group, cores, rows), spots, flat, value_grads[:, 0].reshape(toks, kvw), master[0]
    )
    mine = exchange(blocks, "x").reshape(all_toks, cores * half + kvw)
    weights_old = lax.all_gather(weights_old, "zhi", axis=0, tiled=True)
    mine, weights_old = together(mine, weights_old)

    other = local(
        functools.partial(other_kernel, half),
        [shape((half, kvw), bf16)],
        spots,
        mine,
        own_gain[half:, None],
    )[0]
    came = swap_cores(other)
    own = local(
        functools.partial(own_kernel, half),
        [shape((half, kvw), f32)],
        spots,
        mine,
        own_gain[:half, None],
        after=[other],
    )[0]
    partial = local(add_kernel, [shape((half, kvw), bf16)], spots, own, came)[0]
    grad = lax.psum_scatter(partial, "zhi", scatter_dimension=0, tiled=True)
    weights_other = swap_cores(weights_old)

    mixed, sums = local(
        functools.partial(upstream_kernel, half),
        [shape((all_toks, cores * half), f32), shape((group, 8, all_toks), f32)],
        spots,
        mine,
        weights_old,
        weights_other,
        own_gain[None],
        after=[partial],
    )
    sums = exchange(sums, "x")
    parts = local(
        functools.partial(branch_kernel, (far, rows, width)),
        [shape((layers_y, all_toks, cores * rows), bf16)],
        spots,
        mine,
        mixed,
        sums,
    )[0]
    next_flat, parts = together(next_acts[:, 0].reshape(toks, width), parts)
    came = exchange(parts, "y")

    fresh_blocks = local(
        functools.partial(fresh_kernel, (far, group, cores, rows)),
        [shape((toks, cores * half), bf16)] * group,
        spots,
        reward_ids,
        next_flat,
        norm_gain,
        reward_table,
        scratch=[pltpu.VMEM((toks, width), bf16)],
    )
    fresh_normed = shift(fresh_blocks, "x")

    top_shape = shape((all_toks, cores * rows), bf16)
    top = local(top_kernel, [top_shape], spots, came, after=fresh_blocks[:1])[0]
    behind = [from_behind(top, "zlo", 1)]
    pair = local(pair_kernel, [top_shape], spots, top, behind[0])[0]
    behind.append(from_behind(pair, "zlo", 2))

    first_axes = ("zlo", "zhi")
    last_axes = ("y", "x", "core")
    tile = (8, 128)
    squares = local(
        squares_kernel, [shape((lax.axis_size(first_axes),) + tile, f32)], spots, grad, after=[top] + fresh_normed[1:]
    )[0]
    squares = exchange(squares, first_axes)
    squares = local(relay_kernel, [shape((lax.axis_size(last_axes),) + tile, f32)], spots, squares)[0]
    squares = exchange(squares, last_axes)
    suffix = local(
        functools.partial(suffix_kernel, group),
        [shape((layers_y * group, toks, cores * rows), bf16)],
        spots,
        came,
        *behind,
    )[0]
    shard = shape((rows, kvw), f32)
    moment1_new, moment2_new, weights_new = local(
        functools.partial(adam_kernel, lax.axis_size(section) * width * kvw),
        [shard, shard, shape((rows, kvw), bf16)],
        spots,
        squares,
        grad,
        master[0],
        moment1[0],
        moment2[0],
        after=[suffix],
    )
    weights_new, suffix = together(weights_new, suffix)
    weights_new = lax.all_gather(weights_new, "zhi", axis=0, tiled=True)
    back = exchange(suffix, ("y", "x"))

    weights_other = swap_cores(weights_new)
    first = local(
        functools.partial(first_kernel, half),
        [shape((group, toks, kvw), f32)],
        spots,
        *fresh_normed,
        weights_new,
    )[0]
    fresh = local(
        functools.partial(second_kernel, half),
        [shape((group, toks, kvw), bf16)],
        spots,
        *fresh_normed,
        weights_other,
        first,
    )[0]
    fresh, back = together(fresh, back)
    fresh = jnp.sum(exchange(fresh, "x").astype(f32), axis=0).astype(bf16)
    fresh_values = fresh.reshape(micro, 1, tok_dev, kvw)

    input_grads = local(
        functools.partial(join_kernel, rows), [shape((toks, width), bf16)], spots, back
    )[0].reshape(micro, 1, tok_dev, width)
    return (input_grads, moment1_new[None], moment2_new[None], fresh_values)


def solution(mesh):
    fine = Mesh(mesh.devices.reshape(factors["section"] + factors["dp"]), axes)
    return jax.shard_map(
        per_device,
        mesh=fine,
        in_specs=(
            P(None, section, dp, None),
            P(section, None),
            P(None, section, dp, None),
            P(section, dp, None),
            P(section, dp, None),
            P(section, dp, None),
            P(None, section, dp, None),
            P(),
            P(),
        ),
        out_specs=(
            P(None, section, dp, None),
            P(section, dp, None),
            P(section, dp, None),
            P(None, section, dp, None),
        ),
        check_vma=False,
    )
```

```python
import functools

import jax
import jax.numpy as jnp
from jax import lax
from jax.experimental import pallas as pl
from jax.experimental.pallas import tpu as pltpu
from jax.sharding import Mesh
from jax.sharding import PartitionSpec as P

rms_epsilon = 1e-05
clip_level = 1.0
beta_first = 0.9
beta_second = 0.95
learn_rate = 0.001
decay_rate = 0.01
adam_epsilon = 1e-08
bias_first = 1.0 - 0.9**10
bias_second = 1.0 - 0.95**10

factors = {"section": (4, 4), "dp": (4, 4, 2)}
axes = ("zlo", "y", "zhi", "x", "core")
section = ("zlo", "y")
dp = ("zhi", "x", "core")
near = ("x", "core")
heavy = 2 * 10**10
f32 = jnp.float32
bf16 = jnp.bfloat16


def exchange(blocks, axis):
    return lax.all_to_all(blocks, axis, 0, 0)


def shifts(size):
    return sorted(range(1, size), key=lambda k: -min(k, size - k))


def shift(parts, axis):
    size = len(parts)
    came = [parts[0]] + [None] * (size - 1)
    for k in shifts(size):
        came[k] = lax.ppermute(parts[k], axis, [(i, (i + k) % size) for i in range(size)])
    return came


def swap_cores(block):
    return lax.ppermute(block, "core", [(0, 1), (1, 0)])


def from_behind(block, axis, distance):
    size = lax.axis_size(axis)
    return lax.ppermute(block, axis, [(i + distance, i) for i in range(size - distance)])


def together(*values):
    return lax.optimization_barrier(values)


def inverse_rms(floats):
    return lax.rsqrt(jnp.mean(floats * floats, axis=-1, keepdims=True) + rms_epsilon)


def local(kernel, out_shapes, *arrays, weight=0, scratch=(), after=()):
    def body(*refs):
        kernel(*refs[: len(arrays)], *refs[len(arrays) + len(after) :])

    return pl.pallas_call(
        body,
        out_shape=out_shapes,
        in_specs=[
            pl.BlockSpec(memory_space=pltpu.SMEM if a.dtype == jnp.int32 else pltpu.VMEM)
            for a in arrays
        ]
        + [pl.BlockSpec(memory_space=pl.ANY)] * len(after),
        out_specs=[pl.BlockSpec(memory_space=pltpu.VMEM)] * len(out_shapes),
        scratch_shapes=scratch,
        compiler_params=pltpu.CompilerParams(vmem_limit_bytes=48 * 1024 * 1024),
        cost_estimate=pl.CostEstimate(flops=weight, bytes_accessed=0, transcendentals=0),
    )(*arrays, *after)


def strip_at(start, rows):
    return pl.ds(pl.multiple_of(start, rows), rows)


def split_kernel(sizes, acts, values, master, out, weights):
    far, group, cores, rows = sizes
    core = lax.axis_index("core")
    half = far * rows
    weights[...] = master[...].astype(bf16)
    floats = acts[...].astype(f32)
    scaled = (values[...].astype(f32) * inverse_rms(floats)).astype(bf16)
    for x in range(group):
        for z in range(far):
            for c in range(cores):
                start = ((z * group + x) * cores + ((core + c) & (cores - 1))) * rows
                out[x, :, c * half + z * rows : c * half + (z + 1) * rows] = acts[
                    :, strip_at(start, rows)
                ]
        out[x, :, cores * half :] = scaled


def split(sizes, acts, values, master):
    far, group, cores, rows = sizes
    toks, width = acts.shape
    kvw = values.shape[1]
    steps = 4
    cut = toks // steps
    lanes = cores * far * rows + kvw
    return pl.pallas_call(
        functools.partial(split_kernel, sizes),
        grid=(steps,),
        out_shape=[
            jax.ShapeDtypeStruct((group, toks, lanes), bf16),
            jax.ShapeDtypeStruct((rows, kvw), bf16),
        ],
        in_specs=[
            pl.BlockSpec((cut, width), lambda i: (i, 0)),
            pl.BlockSpec((cut, kvw), lambda i: (i, 0)),
            pl.BlockSpec((rows // steps, kvw), lambda i: (i, 0)),
        ],
        out_specs=[
            pl.BlockSpec((group, cut, lanes), lambda i: (0, i, 0)),
            pl.BlockSpec((rows // steps, kvw), lambda i: (i, 0)),
        ],
        compiler_params=pltpu.CompilerParams(vmem_limit_bytes=63 * 1024 * 1024),
        cost_estimate=pl.CostEstimate(flops=0, bytes_accessed=0, transcendentals=0),
    )(acts, values, master)


def other_kernel(half, mine, gain, out):
    left = mine[:, half : 2 * half]
    part = lax.dot_general(
        left, mine[:, 2 * half :], (((0,), (0,)), ((), ())), preferred_element_type=f32
    )
    out[...] = (part * gain[...]).astype(bf16)


def own_kernel(half, mine, gain, out):
    part = lax.dot_general(
        mine[:, :half], mine[:, 2 * half :], (((0,), (0,)), ((), ())), preferred_element_type=f32
    )
    out[...] = part * gain[...]


def add_kernel(own, came, out):
    out[...] = (own[...] + came[...].astype(f32)).astype(bf16)


def upstream_kernel(half, mine, own, other, gain, mixed, sums):
    values = mine[:, 2 * half :]
    squares, products = 0.0, 0.0
    for c, weights in enumerate((own, other)):
        cols = slice(c * half, (c + 1) * half)
        part = lax.dot_general(
            values, weights[...], (((1,), (1,)), ((), ())), preferred_element_type=f32
        )
        part = part * gain[:, cols]
        mixed[:, cols] = part
        floats = mine[:, cols].astype(f32)
        squares = squares + jnp.sum(floats * floats, axis=1, keepdims=True)
        products = products + jnp.sum(floats * part, axis=1, keepdims=True)
    lane = lax.broadcasted_iota(jnp.int32, (mine.shape[0], 128), 1)
    both = jnp.where(lane == 0, squares, jnp.where(lane == 1, products, 0.0))
    for x in range(sums.shape[0]):
        sums[x] = both.T[:8]


def branch_kernel(sizes, mine, mixed, sums, out):
    far, rows, width = sizes
    half = far * rows
    both = jnp.concatenate([jnp.sum(sums[...], axis=0)] * 16, axis=0).T
    inv = lax.rsqrt(both[:, 0:1] / width + rms_epsilon)
    pull = inv * (inv * (both[:, 1:2] / width))
    for z in range(far):
        for c in range(mixed.shape[1] // half):
            cols = slice(c * half + z * rows, c * half + (z + 1) * rows)
            block = mixed[:, cols] - mine[:, cols].astype(f32) * pull
            out[z, :, c * rows : (c + 1) * rows] = block.astype(bf16)


def fresh_kernel(sizes, ids, acts, gain, table, *refs):
    *outs, normed = refs
    far, group, cores, rows = sizes
    micro = ids.shape[0]
    half = far * rows
    floats = acts[...].astype(f32)
    toks = floats.shape[0]
    row = lax.broadcasted_iota(jnp.int32, (toks, 1), 0)
    for m in range(micro):
        bin_id = ids[m, lax.axis_index(dp)]
        embed = jnp.zeros((1, floats.shape[1]), f32)
        for b in range(table.shape[0]):
            embed = jnp.where(bin_id == b, table[b : b + 1, :].astype(f32), embed)
        first = jnp.logical_and(row == m * (toks // micro), lax.axis_index(section) == 0)
        floats = jnp.where(first, embed, floats)
    normed[...] = (floats * inverse_rms(floats) * gain[...]).astype(bf16)
    for k, out in enumerate(outs):
        x = (lax.axis_index("x") + k) & (group - 1)
        for z in range(far):
            for c in range(cores):
                start = ((z * group + x) * cores + ((lax.axis_index("core") + c) & (cores - 1))) * rows
                out[:, c * half + z * rows : c * half + (z + 1) * rows] = normed[
                    :, strip_at(start, rows)
                ]


def first_kernel(half, *refs):
    *blocks, weights, out = refs
    for k, block in enumerate(blocks):
        part = jnp.dot(block[:, :half], weights[...], preferred_element_type=f32)
        out[(lax.axis_index("x") - k) & (len(blocks) - 1)] = part


def second_kernel(half, *refs):
    *blocks, weights, first, out = refs
    for k, block in enumerate(blocks):
        x = (lax.axis_index("x") - k) & (len(blocks) - 1)
        part = jnp.dot(block[:, half:], weights[...], preferred_element_type=f32)
        out[x] = (first[x] + part).astype(bf16)


def top_kernel(came, out):
    out[...] = jnp.sum(came[...].astype(f32), axis=0).astype(bf16)


def pair_kernel(top, behind, out):
    out[...] = (top[...].astype(f32) + behind[...].astype(f32)).astype(bf16)


def suffix_kernel(group, came, *refs):
    *parts, out = refs
    block = sum(part[...].astype(f32) for part in parts)
    toks = out.shape[1]
    for layer in reversed(range(came.shape[0])):
        block = block + came[layer].astype(f32)
        for x in range(group):
            out[layer * group + x] = block[x * toks : (x + 1) * toks].astype(bf16)


def squares_kernel(grad, out):
    floats = grad[...].astype(f32)
    out[...] = jnp.broadcast_to(jnp.sum(floats * floats), out.shape)


def relay_kernel(sums, out):
    out[...] = jnp.broadcast_to(jnp.sum(sums[...], axis=0, keepdims=True), out.shape)


def adam_kernel(entries, sums, grad, master, first, second, first_new, second_new, weights):
    squares = jnp.sum(sums[...], axis=0)
    clip = jnp.minimum(1.0, clip_level / jnp.sqrt(squares / entries + 1e-12))[0:1, 0:1]
    clipped = grad[...].astype(f32) * clip
    moment1 = beta_first * first[...] + (1.0 - beta_first) * clipped
    moment2 = beta_second * second[...] + (1.0 - beta_second) * clipped * clipped
    first_new[...] = moment1
    second_new[...] = moment2
    update = (
        moment1 / bias_first / (jnp.sqrt(moment2 / bias_second) + adam_epsilon)
        + decay_rate * master[...]
    )
    weights[...] = (master[...] - learn_rate * update).astype(bf16)


def join_kernel(rows, back, out):
    cores = back.shape[2] // rows
    for j in range(back.shape[0]):
        for c in range(cores):
            start = (j * cores + ((lax.axis_index("core") + c) & (cores - 1))) * rows
            out[:, strip_at(start, rows)] = back[j, :, c * rows : (c + 1) * rows]


def per_device(
    acts, norm_gain, value_grads, master, moment1, moment2, next_acts, reward_table, reward_ids
):
    micro, _, tok_dev, width = acts.shape
    kvw = value_grads.shape[3]
    toks = micro * tok_dev
    far = lax.axis_size("zhi")
    group = lax.axis_size("x")
    cores = lax.axis_size("core")
    layers_y = lax.axis_size("y")
    rows = width // (far * group * cores)
    half = far * rows
    all_toks = group * toks
    core, spot_x = lax.axis_index("core"), lax.axis_index("x")
    shape = jax.ShapeDtypeStruct
    gain = norm_gain[0]

    def of_features(block):
        split = block.reshape(block.shape[:-1] + (far, group, cores, rows))
        split = lax.dynamic_index_in_dim(split, spot_x, split.ndim - 3, False)
        halves = [
            lax.dynamic_index_in_dim(split, core ^ c, split.ndim - 2, False) for c in range(cores)
        ]
        return jnp.concatenate([h.reshape(block.shape[:-1] + (half,)) for h in halves], axis=-1)

    own_gain = of_features(gain)

    flat = acts[:, 0].reshape(toks, width)
    blocks, weights_old = split(
        (far, group, cores, rows), flat, value_grads[:, 0].reshape(toks, kvw), master[0]
    )
    mine = exchange(blocks, "x").reshape(all_toks, cores * half + kvw)
    weights_old = lax.all_gather(weights_old, "zhi", axis=0, tiled=True)
    mine, weights_old = together(mine, weights_old)

    other = local(
        functools.partial(other_kernel, half),
        [shape((half, kvw), bf16)],
        mine,
        own_gain[half:, None],
    )[0]
    came = swap_cores(other)
    own = local(
        functools.partial(own_kernel, half),
        [shape((half, kvw), f32)],
        mine,
        own_gain[:half, None],
        after=[other],
    )[0]
    partial = local(add_kernel, [shape((half, kvw), bf16)], own, came)[0]
    grad = lax.psum_scatter(partial, "zhi", scatter_dimension=0, tiled=True)
    weights_other = swap_cores(weights_old)

    mixed, sums = local(
        functools.partial(upstream_kernel, half),
        [shape((all_toks, cores * half), f32), shape((group, 8, all_toks), f32)],
        mine,
        weights_old,
        weights_other,
        own_gain[None],
        after=[partial],
    )
    sums = exchange(sums, "x")
    parts = local(
        functools.partial(branch_kernel, (far, rows, width)),
        [shape((layers_y, all_toks, cores * rows), bf16)],
        mine,
        mixed,
        sums,
    )[0]
    next_flat, parts = together(next_acts[:, 0].reshape(toks, width), parts)
    came = exchange(parts, "y")

    fresh_blocks = local(
        functools.partial(fresh_kernel, (far, group, cores, rows)),
        [shape((toks, cores * half), bf16)] * group,
        reward_ids,
        next_flat,
        norm_gain,
        reward_table,
        scratch=[pltpu.VMEM((toks, width), bf16)],
    )
    fresh_normed = shift(fresh_blocks, "x")

    top_shape = shape((all_toks, cores * rows), bf16)
    top = local(top_kernel, [top_shape], came, after=fresh_blocks[:1])[0]
    behind = [from_behind(top, "zlo", 1)]
    pair = local(pair_kernel, [top_shape], top, behind[0])[0]
    behind.append(from_behind(pair, "zlo", 2))

    first_axes = ("zlo", "zhi")
    last_axes = ("y", "x", "core")
    tile = (8, 128)
    squares = local(
        squares_kernel, [shape((lax.axis_size(first_axes),) + tile, f32)], grad, after=[top] + fresh_normed[1:]
    )[0]
    squares = exchange(squares, first_axes)
    squares = local(relay_kernel, [shape((lax.axis_size(last_axes),) + tile, f32)], squares)[0]
    squares = exchange(squares, last_axes)
    suffix = local(
        functools.partial(suffix_kernel, group),
        [shape((layers_y * group, toks, cores * rows), bf16)],
        came,
        *behind,
    )[0]
    shard = shape((rows, kvw), f32)
    moment1_new, moment2_new, weights_new = local(
        functools.partial(adam_kernel, lax.axis_size(section) * width * kvw),
        [shard, shard, shape((rows, kvw), bf16)],
        squares,
        grad,
        master[0],
        moment1[0],
        moment2[0],
        after=[suffix],
    )
    weights_new, suffix = together(weights_new, suffix)
    weights_new = lax.all_gather(weights_new, "zhi", axis=0, tiled=True)
    back = exchange(suffix, ("y", "x"))

    weights_other = swap_cores(weights_new)
    first = local(
        functools.partial(first_kernel, half),
        [shape((group, toks, kvw), f32)],
        *fresh_normed,
        weights_new,
    )[0]
    fresh = local(
        functools.partial(second_kernel, half),
        [shape((group, toks, kvw), bf16)],
        *fresh_normed,
        weights_other,
        first,
    )[0]
    fresh, back = together(fresh, back)
    fresh = jnp.sum(exchange(fresh, "x").astype(f32), axis=0).astype(bf16)
    fresh_values = fresh.reshape(micro, 1, tok_dev, kvw)

    input_grads = local(
        functools.partial(join_kernel, rows), [shape((toks, width), bf16)], back
    )[0].reshape(micro, 1, tok_dev, width)
    return (input_grads, moment1_new[None], moment2_new[None], fresh_values)


def solution(mesh):
    fine = Mesh(mesh.devices.reshape(factors["section"] + factors["dp"]), axes)
    return jax.shard_map(
        per_device,
        mesh=fine,
        in_specs=(
            P(None, section, dp, None),
            P(section, None),
            P(None, section, dp, None),
            P(section, dp, None),
            P(section, dp, None),
            P(section, dp, None),
            P(None, section, dp, None),
            P(),
            P(),
        ),
        out_specs=(
            P(None, section, dp, None),
            P(section, dp, None),
            P(section, dp, None),
            P(None, section, dp, None),
        ),
        check_vma=False,
    )
```

```python
import functools

import jax
import jax.numpy as jnp
from jax import lax
from jax.experimental import pallas as pl
from jax.experimental.pallas import tpu as pltpu
from jax.sharding import Mesh
from jax.sharding import PartitionSpec as P

rms_epsilon = 1e-05
clip_level = 1.0
beta_first = 0.9
beta_second = 0.95
learn_rate = 0.001
decay_rate = 0.01
adam_epsilon = 1e-08
bias_first = 1.0 - 0.9**10
bias_second = 1.0 - 0.95**10

factors = {"section": (4, 4), "dp": (4, 4, 2)}
axes = ("zlo", "y", "zhi", "x", "core")
section = ("zlo", "y")
dp = ("zhi", "x", "core")
near = ("x", "core")
heavy = 2 * 10**10
f32 = jnp.float32
bf16 = jnp.bfloat16


def exchange(blocks, axis):
    return lax.all_to_all(blocks, axis, 0, 0)


def shifts(size):
    return sorted(range(1, size), key=lambda k: -min(k, size - k))


def shift(parts, axis):
    size = len(parts)
    came = [parts[0]] + [None] * (size - 1)
    for k in shifts(size):
        came[k] = lax.ppermute(parts[k], axis, [(i, (i + k) % size) for i in range(size)])
    return came


def swap_cores(block):
    return lax.ppermute(block, "core", [(0, 1), (1, 0)])


def from_behind(block, axis, distance):
    size = lax.axis_size(axis)
    return lax.ppermute(block, axis, [(i + distance, i) for i in range(size - distance)])


def together(*values):
    return lax.optimization_barrier(values)


def inverse_rms(floats):
    return lax.rsqrt(jnp.mean(floats * floats, axis=-1, keepdims=True) + rms_epsilon)


def local(kernel, out_shapes, *arrays, weight=0, scratch=(), after=()):
    def body(*refs):
        kernel(*refs[: len(arrays)], *refs[len(arrays) + len(after) :])

    return pl.pallas_call(
        body,
        out_shape=out_shapes,
        in_specs=[
            pl.BlockSpec(memory_space=pltpu.SMEM if a.dtype == jnp.int32 else pltpu.VMEM)
            for a in arrays
        ]
        + [pl.BlockSpec(memory_space=pl.ANY)] * len(after),
        out_specs=[pl.BlockSpec(memory_space=pltpu.VMEM)] * len(out_shapes),
        scratch_shapes=scratch,
        compiler_params=pltpu.CompilerParams(vmem_limit_bytes=48 * 1024 * 1024),
        cost_estimate=pl.CostEstimate(flops=weight, bytes_accessed=0, transcendentals=0),
    )(*arrays, *after)


def strip_at(start, rows):
    return pl.ds(pl.multiple_of(start, rows), rows)


def split_kernel(sizes, acts, values, master, out, weights):
    far, group, cores, rows = sizes
    core = lax.axis_index("core")
    half = far * rows
    weights[...] = master[...].astype(bf16)
    floats = acts[...].astype(f32)
    scaled = (values[...].astype(f32) * inverse_rms(floats)).astype(bf16)
    for x in range(group):
        for z in range(far):
            for c in range(cores):
                start = ((z * group + x) * cores + ((core + c) & (cores - 1))) * rows
                out[x, :, c * half + z * rows : c * half + (z + 1) * rows] = acts[
                    :, strip_at(start, rows)
                ]
        out[x, :, cores * half :] = scaled


def split(sizes, acts, values, master):
    far, group, cores, rows = sizes
    toks, width = acts.shape
    kvw = values.shape[1]
    steps = 4
    cut = toks // steps
    lanes = cores * far * rows + kvw
    return pl.pallas_call(
        functools.partial(split_kernel, sizes),
        grid=(steps,),
        out_shape=[
            jax.ShapeDtypeStruct((group, toks, lanes), bf16),
            jax.ShapeDtypeStruct((rows, kvw), bf16),
        ],
        in_specs=[
            pl.BlockSpec((cut, width), lambda i: (i, 0)),
            pl.BlockSpec((cut, kvw), lambda i: (i, 0)),
            pl.BlockSpec((rows // steps, kvw), lambda i: (i, 0)),
        ],
        out_specs=[
            pl.BlockSpec((group, cut, lanes), lambda i: (0, i, 0)),
            pl.BlockSpec((rows // steps, kvw), lambda i: (i, 0)),
        ],
        compiler_params=pltpu.CompilerParams(vmem_limit_bytes=63 * 1024 * 1024),
        cost_estimate=pl.CostEstimate(flops=0, bytes_accessed=0, transcendentals=0),
    )(acts, values, master)


def other_kernel(half, mine, gain, out):
    left = mine[:, half : 2 * half]
    part = lax.dot_general(
        left, mine[:, 2 * half :], (((0,), (0,)), ((), ())), preferred_element_type=f32
    )
    out[...] = (part * gain[...]).astype(bf16)


def own_kernel(half, mine, gain, out):
    part = lax.dot_general(
        mine[:, :half], mine[:, 2 * half :], (((0,), (0,)), ((), ())), preferred_element_type=f32
    )
    out[...] = part * gain[...]


def add_kernel(own, came, out):
    out[...] = (own[...] + came[...].astype(f32)).astype(bf16)


def upstream_kernel(half, mine, own, other, gain, mixed, sums):
    values = mine[:, 2 * half :]
    squares, products = 0.0, 0.0
    for c, weights in enumerate((own, other)):
        cols = slice(c * half, (c + 1) * half)
        part = lax.dot_general(
            values, weights[...], (((1,), (1,)), ((), ())), preferred_element_type=f32
        )
        part = part * gain[:, cols]
        mixed[:, cols] = part
        floats = mine[:, cols].astype(f32)
        squares = squares + jnp.sum(floats * floats, axis=1, keepdims=True)
        products = products + jnp.sum(floats * part, axis=1, keepdims=True)
    lane = lax.broadcasted_iota(jnp.int32, (mine.shape[0], 128), 1)
    both = jnp.where(lane == 0, squares, jnp.where(lane == 1, products, 0.0))
    for x in range(sums.shape[0]):
        sums[x] = both.T[:8]


def branch_kernel(sizes, mine, mixed, sums, out):
    far, rows, width = sizes
    half = far * rows
    both = jnp.concatenate([jnp.sum(sums[...], axis=0)] * 16, axis=0).T
    inv = lax.rsqrt(both[:, 0:1] / width + rms_epsilon)
    pull = inv * (inv * (both[:, 1:2] / width))
    for z in range(far):
        for c in range(mixed.shape[1] // half):
            cols = slice(c * half + z * rows, c * half + (z + 1) * rows)
            block = mixed[:, cols] - mine[:, cols].astype(f32) * pull
            out[z, :, c * rows : (c + 1) * rows] = block.astype(bf16)


def fresh_kernel(sizes, ids, acts, gain, table, *refs):
    *outs, normed = refs
    far, group, cores, rows = sizes
    micro = ids.shape[0]
    half = far * rows
    floats = acts[...].astype(f32)
    toks = floats.shape[0]
    row = lax.broadcasted_iota(jnp.int32, (toks, 1), 0)
    for m in range(micro):
        bin_id = ids[m, lax.axis_index(dp)]
        embed = jnp.zeros((1, floats.shape[1]), f32)
        for b in range(table.shape[0]):
            embed = jnp.where(bin_id == b, table[b : b + 1, :].astype(f32), embed)
        first = jnp.logical_and(row == m * (toks // micro), lax.axis_index(section) == 0)
        floats = jnp.where(first, embed, floats)
    normed[...] = (floats * inverse_rms(floats) * gain[...]).astype(bf16)
    for k, out in enumerate(outs):
        x = (lax.axis_index("x") + k) & (group - 1)
        for z in range(far):
            for c in range(cores):
                start = ((z * group + x) * cores + ((lax.axis_index("core") + c) & (cores - 1))) * rows
                out[:, c * half + z * rows : c * half + (z + 1) * rows] = normed[
                    :, strip_at(start, rows)
                ]


def first_kernel(half, *refs):
    *blocks, weights, out = refs
    for k, block in enumerate(blocks):
        part = jnp.dot(block[:, :half], weights[...], preferred_element_type=f32)
        out[(lax.axis_index("x") - k) & (len(blocks) - 1)] = part


def second_kernel(half, *refs):
    *blocks, weights, first, out = refs
    for k, block in enumerate(blocks):
        x = (lax.axis_index("x") - k) & (len(blocks) - 1)
        part = jnp.dot(block[:, half:], weights[...], preferred_element_type=f32)
        out[x] = (first[x] + part).astype(bf16)


def top_kernel(came, out):
    out[...] = jnp.sum(came[...].astype(f32), axis=0).astype(bf16)


def pair_kernel(top, behind, out):
    out[...] = (top[...].astype(f32) + behind[...].astype(f32)).astype(bf16)


def suffix_kernel(group, came, *refs):
    *parts, out = refs
    block = sum(part[...].astype(f32) for part in parts)
    toks = out.shape[1]
    for layer in reversed(range(came.shape[0])):
        block = block + came[layer].astype(f32)
        for x in range(group):
            out[layer * group + x] = block[x * toks : (x + 1) * toks].astype(bf16)


def squares_kernel(grad, out):
    floats = grad[...].astype(f32)
    out[...] = jnp.broadcast_to(jnp.sum(floats * floats), out.shape)


def relay_kernel(sums, out):
    out[...] = jnp.broadcast_to(jnp.sum(sums[...], axis=0, keepdims=True), out.shape)


def adam_kernel(entries, sums, grad, master, first, second, first_new, second_new, weights):
    squares = jnp.sum(sums[...], axis=0)
    clip = jnp.minimum(1.0, clip_level / jnp.sqrt(squares / entries + 1e-12))[0:1, 0:1]
    clipped = grad[...].astype(f32) * clip
    moment1 = beta_first * first[...] + (1.0 - beta_first) * clipped
    moment2 = beta_second * second[...] + (1.0 - beta_second) * clipped * clipped
    first_new[...] = moment1
    second_new[...] = moment2
    update = (
        moment1 / bias_first / (jnp.sqrt(moment2 / bias_second) + adam_epsilon)
        + decay_rate * master[...]
    )
    weights[...] = (master[...] - learn_rate * update).astype(bf16)


def join_kernel(rows, back, out):
    cores = back.shape[2] // rows
    for j in range(back.shape[0]):
        for c in range(cores):
            start = (j * cores + ((lax.axis_index("core") + c) & (cores - 1))) * rows
            out[:, strip_at(start, rows)] = back[j, :, c * rows : (c + 1) * rows]


def per_device(
    acts, norm_gain, value_grads, master, moment1, moment2, next_acts, reward_table, reward_ids
):
    micro, _, tok_dev, width = acts.shape
    kvw = value_grads.shape[3]
    toks = micro * tok_dev
    far = lax.axis_size("zhi")
    group = lax.axis_size("x")
    cores = lax.axis_size("core")
    layers_y = lax.axis_size("y")
    rows = width // (far * group * cores)
    half = far * rows
    all_toks = group * toks
    core, spot_x = lax.axis_index("core"), lax.axis_index("x")
    shape = jax.ShapeDtypeStruct
    gain = norm_gain[0]

    def of_features(block):
        split = block.reshape(block.shape[:-1] + (far, group, cores, rows))
        split = lax.dynamic_index_in_dim(split, spot_x, split.ndim - 3, False)
        halves = [
            lax.dynamic_index_in_dim(split, core ^ c, split.ndim - 2, False) for c in range(cores)
        ]
        return jnp.concatenate([h.reshape(block.shape[:-1] + (half,)) for h in halves], axis=-1)

    own_gain = of_features(gain)

    flat = acts[:, 0].reshape(toks, width)
    blocks, weights_old = split(
        (far, group, cores, rows), flat, value_grads[:, 0].reshape(toks, kvw), master[0]
    )
    mine = exchange(blocks, "x").reshape(all_toks, cores * half + kvw)
    weights_old = lax.all_gather(weights_old, "zhi", axis=0, tiled=True)
    mine, weights_old = together(mine, weights_old)

    other = local(
        functools.partial(other_kernel, half),
        [shape((half, kvw), bf16)],
        mine,
        own_gain[half:, None],
    )[0]
    came = swap_cores(other)
    own = local(
        functools.partial(own_kernel, half),
        [shape((half, kvw), f32)],
        mine,
        own_gain[:half, None],
        after=[other],
    )[0]
    partial = local(add_kernel, [shape((half, kvw), bf16)], own, came)[0]
    grad = lax.psum_scatter(partial, "zhi", scatter_dimension=0, tiled=True)
    weights_other = swap_cores(weights_old)

    mixed, sums = local(
        functools.partial(upstream_kernel, half),
        [shape((all_toks, cores * half), f32), shape((group, 8, all_toks), f32)],
        mine,
        weights_old,
        weights_other,
        own_gain[None],
        after=[partial],
    )
    sums = exchange(sums, "x")
    parts = local(
        functools.partial(branch_kernel, (far, rows, width)),
        [shape((layers_y, all_toks, cores * rows), bf16)],
        mine,
        mixed,
        sums,
    )[0]
    next_flat, parts = together(next_acts[:, 0].reshape(toks, width), parts)
    came = exchange(parts, "y")

    fresh_blocks = local(
        functools.partial(fresh_kernel, (far, group, cores, rows)),
        [shape((toks, cores * half), bf16)] * group,
        reward_ids,
        next_flat,
        norm_gain,
        reward_table,
        scratch=[pltpu.VMEM((toks, width), bf16)],
    )
    fresh_normed = shift(fresh_blocks, "x")

    top_shape = shape((all_toks, cores * rows), bf16)
    top = local(top_kernel, [top_shape], came, after=fresh_blocks[:1])[0]
    behind = [from_behind(top, "zlo", 1)]

    first_axes = ("zlo", "zhi")
    last_axes = ("y", "x", "core")
    tile = (8, 128)
    squares = local(
        squares_kernel, [shape((lax.axis_size(first_axes),) + tile, f32)], grad, after=[top] + fresh_normed[1:]
    )[0]
    squares = exchange(squares, first_axes)
    pair = local(pair_kernel, [top_shape], top, behind[0], after=[squares])[0]
    behind.append(from_behind(pair, "zlo", 2))
    squares = local(relay_kernel, [shape((lax.axis_size(last_axes),) + tile, f32)], squares)[0]
    squares = exchange(squares, last_axes)
    suffix = local(
        functools.partial(suffix_kernel, group),
        [shape((layers_y * group, toks, cores * rows), bf16)],
        came,
        *behind,
    )[0]
    shard = shape((rows, kvw), f32)
    moment1_new, moment2_new, weights_new = local(
        functools.partial(adam_kernel, lax.axis_size(section) * width * kvw),
        [shard, shard, shape((rows, kvw), bf16)],
        squares,
        grad,
        master[0],
        moment1[0],
        moment2[0],
        after=[suffix],
    )
    weights_new, suffix = together(weights_new, suffix)
    weights_new = lax.all_gather(weights_new, "zhi", axis=0, tiled=True)
    back = exchange(suffix, ("y", "x"))

    weights_other = swap_cores(weights_new)
    first = local(
        functools.partial(first_kernel, half),
        [shape((group, toks, kvw), f32)],
        *fresh_normed,
        weights_new,
    )[0]
    fresh = local(
        functools.partial(second_kernel, half),
        [shape((group, toks, kvw), bf16)],
        *fresh_normed,
        weights_other,
        first,
    )[0]
    fresh, back = together(fresh, back)
    fresh = jnp.sum(exchange(fresh, "x").astype(f32), axis=0).astype(bf16)
    fresh_values = fresh.reshape(micro, 1, tok_dev, kvw)

    input_grads = local(
        functools.partial(join_kernel, rows), [shape((toks, width), bf16)], back
    )[0].reshape(micro, 1, tok_dev, width)
    return (input_grads, moment1_new[None], moment2_new[None], fresh_values)


def solution(mesh):
    fine = Mesh(mesh.devices.reshape(factors["section"] + factors["dp"]), axes)
    return jax.shard_map(
        per_device,
        mesh=fine,
        in_specs=(
            P(None, section, dp, None),
            P(section, None),
            P(None, section, dp, None),
            P(section, dp, None),
            P(section, dp, None),
            P(section, dp, None),
            P(None, section, dp, None),
            P(),
            P(),
        ),
        out_specs=(
            P(None, section, dp, None),
            P(section, dp, None),
            P(section, dp, None),
            P(None, section, dp, None),
        ),
        check_vma=False,
    )
```

```python
import functools

import jax
import jax.numpy as jnp
from jax import lax
from jax.experimental import pallas as pl
from jax.experimental.pallas import tpu as pltpu
from jax.sharding import Mesh
from jax.sharding import PartitionSpec as P

rms_epsilon = 1e-05
clip_level = 1.0
beta_first = 0.9
beta_second = 0.95
learn_rate = 0.001
decay_rate = 0.01
adam_epsilon = 1e-08
bias_first = 1.0 - 0.9**10
bias_second = 1.0 - 0.95**10

factors = {"section": (4, 4), "dp": (4, 4, 2)}
axes = ("zlo", "y", "zhi", "x", "core")
section = ("zlo", "y")
dp = ("zhi", "x", "core")
near = ("x", "core")
heavy = 2 * 10**10
f32 = jnp.float32
bf16 = jnp.bfloat16


def exchange(blocks, axis):
    return lax.all_to_all(blocks, axis, 0, 0)


def shifts(size):
    return sorted(range(1, size), key=lambda k: -min(k, size - k))


def shift(parts, axis):
    size = len(parts)
    came = [parts[0]] + [None] * (size - 1)
    for k in shifts(size):
        came[k] = lax.ppermute(parts[k], axis, [(i, (i + k) % size) for i in range(size)])
    return came


def swap_cores(block):
    return lax.ppermute(block, "core", [(0, 1), (1, 0)])


def from_behind(block, axis, distance):
    size = lax.axis_size(axis)
    return lax.ppermute(block, axis, [(i + distance, i) for i in range(size - distance)])


def together(*values):
    return lax.optimization_barrier(values)


def inverse_rms(floats):
    return lax.rsqrt(jnp.mean(floats * floats, axis=-1, keepdims=True) + rms_epsilon)


def local(kernel, out_shapes, *arrays, weight=0, scratch=(), after=()):
    def body(*refs):
        kernel(*refs[: len(arrays)], *refs[len(arrays) + len(after) :])

    return pl.pallas_call(
        body,
        out_shape=out_shapes,
        in_specs=[
            pl.BlockSpec(memory_space=pltpu.SMEM if a.dtype == jnp.int32 else pltpu.VMEM)
            for a in arrays
        ]
        + [pl.BlockSpec(memory_space=pl.ANY)] * len(after),
        out_specs=[pl.BlockSpec(memory_space=pltpu.VMEM)] * len(out_shapes),
        scratch_shapes=scratch,
        compiler_params=pltpu.CompilerParams(vmem_limit_bytes=48 * 1024 * 1024),
        cost_estimate=pl.CostEstimate(flops=weight, bytes_accessed=0, transcendentals=0),
    )(*arrays, *after)


def strip_at(start, rows):
    return pl.ds(pl.multiple_of(start, rows), rows)


def split_kernel(sizes, acts, values, master, out, weights):
    far, group, cores, rows = sizes
    core = lax.axis_index("core")
    half = far * rows
    weights[...] = master[...].astype(bf16)
    floats = acts[...].astype(f32)
    scaled = (values[...].astype(f32) * inverse_rms(floats)).astype(bf16)
    for x in range(group):
        for z in range(far):
            for c in range(cores):
                start = ((z * group + x) * cores + ((core + c) & (cores - 1))) * rows
                out[x, :, c * half + z * rows : c * half + (z + 1) * rows] = acts[
                    :, strip_at(start, rows)
                ]
        out[x, :, cores * half :] = scaled


def split(sizes, acts, values, master):
    far, group, cores, rows = sizes
    toks, width = acts.shape
    kvw = values.shape[1]
    steps = 4
    cut = toks // steps
    lanes = cores * far * rows + kvw
    return pl.pallas_call(
        functools.partial(split_kernel, sizes),
        grid=(steps,),
        out_shape=[
            jax.ShapeDtypeStruct((group, toks, lanes), bf16),
            jax.ShapeDtypeStruct((rows, kvw), bf16),
        ],
        in_specs=[
            pl.BlockSpec((cut, width), lambda i: (i, 0)),
            pl.BlockSpec((cut, kvw), lambda i: (i, 0)),
            pl.BlockSpec((rows // steps, kvw), lambda i: (i, 0)),
        ],
        out_specs=[
            pl.BlockSpec((group, cut, lanes), lambda i: (0, i, 0)),
            pl.BlockSpec((rows // steps, kvw), lambda i: (i, 0)),
        ],
        compiler_params=pltpu.CompilerParams(vmem_limit_bytes=63 * 1024 * 1024),
        cost_estimate=pl.CostEstimate(flops=0, bytes_accessed=0, transcendentals=0),
    )(acts, values, master)


def other_kernel(half, mine, gain, out):
    left = mine[:, half : 2 * half]
    part = lax.dot_general(
        left, mine[:, 2 * half :], (((0,), (0,)), ((), ())), preferred_element_type=f32
    )
    out[...] = (part * gain[...]).astype(bf16)


def own_kernel(half, mine, gain, out):
    part = lax.dot_general(
        mine[:, :half], mine[:, 2 * half :], (((0,), (0,)), ((), ())), preferred_element_type=f32
    )
    out[...] = part * gain[...]


def add_kernel(own, came, out):
    out[...] = (own[...] + came[...].astype(f32)).astype(bf16)


def upstream_kernel(half, mine, own, other, gain, mixed, sums):
    values = mine[:, 2 * half :]
    squares, products = 0.0, 0.0
    for c, weights in enumerate((own, other)):
        cols = slice(c * half, (c + 1) * half)
        part = lax.dot_general(
            values, weights[...], (((1,), (1,)), ((), ())), preferred_element_type=f32
        )
        part = part * gain[:, cols]
        mixed[:, cols] = part
        floats = mine[:, cols].astype(f32)
        squares = squares + jnp.sum(floats * floats, axis=1, keepdims=True)
        products = products + jnp.sum(floats * part, axis=1, keepdims=True)
    lane = lax.broadcasted_iota(jnp.int32, (mine.shape[0], 128), 1)
    both = jnp.where(lane == 0, squares, jnp.where(lane == 1, products, 0.0))
    for x in range(sums.shape[0]):
        sums[x] = both.T[:8]


def branch_kernel(sizes, mine, mixed, sums, out):
    far, rows, width = sizes
    half = far * rows
    both = jnp.concatenate([jnp.sum(sums[...], axis=0)] * 16, axis=0).T
    inv = lax.rsqrt(both[:, 0:1] / width + rms_epsilon)
    pull = inv * (inv * (both[:, 1:2] / width))
    for z in range(far):
        for c in range(mixed.shape[1] // half):
            cols = slice(c * half + z * rows, c * half + (z + 1) * rows)
            block = mixed[:, cols] - mine[:, cols].astype(f32) * pull
            out[z, :, c * rows : (c + 1) * rows] = block.astype(bf16)


def fresh_kernel(sizes, ids, acts, gain, table, *refs):
    *outs, normed = refs
    far, group, cores, rows = sizes
    micro = ids.shape[0]
    half = far * rows
    floats = acts[...].astype(f32)
    toks = floats.shape[0]
    row = lax.broadcasted_iota(jnp.int32, (toks, 1), 0)
    for m in range(micro):
        bin_id = ids[m, lax.axis_index(dp)]
        embed = jnp.zeros((1, floats.shape[1]), f32)
        for b in range(table.shape[0]):
            embed = jnp.where(bin_id == b, table[b : b + 1, :].astype(f32), embed)
        first = jnp.logical_and(row == m * (toks // micro), lax.axis_index(section) == 0)
        floats = jnp.where(first, embed, floats)
    normed[...] = (floats * inverse_rms(floats) * gain[...]).astype(bf16)
    for k, out in enumerate(outs):
        x = (lax.axis_index("x") + k) & (group - 1)
        for z in range(far):
            for c in range(cores):
                start = ((z * group + x) * cores + ((lax.axis_index("core") + c) & (cores - 1))) * rows
                out[:, c * half + z * rows : c * half + (z + 1) * rows] = normed[
                    :, strip_at(start, rows)
                ]


def first_kernel(half, *refs):
    *blocks, weights, out = refs
    for k, block in enumerate(blocks):
        part = jnp.dot(block[:, :half], weights[...], preferred_element_type=f32)
        out[(lax.axis_index("x") - k) & (len(blocks) - 1)] = part


def second_kernel(half, *refs):
    *blocks, weights, first, out = refs
    for k, block in enumerate(blocks):
        x = (lax.axis_index("x") - k) & (len(blocks) - 1)
        part = jnp.dot(block[:, half:], weights[...], preferred_element_type=f32)
        out[x] = (first[x] + part).astype(bf16)


def top_kernel(came, out):
    out[...] = jnp.sum(came[...].astype(f32), axis=0).astype(bf16)


def pair_kernel(top, behind, out):
    out[...] = (top[...].astype(f32) + behind[...].astype(f32)).astype(bf16)


def suffix_kernel(group, came, *refs):
    *parts, out = refs
    block = sum(part[...].astype(f32) for part in parts)
    toks = out.shape[1]
    for layer in reversed(range(came.shape[0])):
        block = block + came[layer].astype(f32)
        for x in range(group):
            out[layer * group + x] = block[x * toks : (x + 1) * toks].astype(bf16)


def squares_kernel(grad, out):
    floats = grad[...].astype(f32)
    out[...] = jnp.broadcast_to(jnp.sum(floats * floats), out.shape)


def relay_kernel(sums, out):
    out[...] = jnp.broadcast_to(jnp.sum(sums[...], axis=0, keepdims=True), out.shape)


def adam_kernel(entries, sums, grad, master, first, second, first_new, second_new, weights):
    squares = jnp.sum(sums[...], axis=0)
    clip = jnp.minimum(1.0, clip_level / jnp.sqrt(squares / entries + 1e-12))[0:1, 0:1]
    clipped = grad[...].astype(f32) * clip
    moment1 = beta_first * first[...] + (1.0 - beta_first) * clipped
    moment2 = beta_second * second[...] + (1.0 - beta_second) * clipped * clipped
    first_new[...] = moment1
    second_new[...] = moment2
    update = (
        moment1 / bias_first / (jnp.sqrt(moment2 / bias_second) + adam_epsilon)
        + decay_rate * master[...]
    )
    weights[...] = (master[...] - learn_rate * update).astype(bf16)


def join_kernel(rows, back, out):
    cores = back.shape[2] // rows
    for j in range(back.shape[0]):
        for c in range(cores):
            start = (j * cores + ((lax.axis_index("core") + c) & (cores - 1))) * rows
            out[:, strip_at(start, rows)] = back[j, :, c * rows : (c + 1) * rows]


def per_device(
    acts, norm_gain, value_grads, master, moment1, moment2, next_acts, reward_table, reward_ids
):
    micro, _, tok_dev, width = acts.shape
    kvw = value_grads.shape[3]
    toks = micro * tok_dev
    far = lax.axis_size("zhi")
    group = lax.axis_size("x")
    cores = lax.axis_size("core")
    layers_y = lax.axis_size("y")
    rows = width // (far * group * cores)
    half = far * rows
    all_toks = group * toks
    core, spot_x = lax.axis_index("core"), lax.axis_index("x")
    shape = jax.ShapeDtypeStruct
    gain = norm_gain[0]

    def of_features(block):
        split = block.reshape(block.shape[:-1] + (far, group, cores, rows))
        split = lax.dynamic_index_in_dim(split, spot_x, split.ndim - 3, False)
        halves = [
            lax.dynamic_index_in_dim(split, core ^ c, split.ndim - 2, False) for c in range(cores)
        ]
        return jnp.concatenate([h.reshape(block.shape[:-1] + (half,)) for h in halves], axis=-1)

    own_gain = of_features(gain)

    flat = acts[:, 0].reshape(toks, width)
    blocks, weights_old = split(
        (far, group, cores, rows), flat, value_grads[:, 0].reshape(toks, kvw), master[0]
    )
    mine = exchange(blocks, "x").reshape(all_toks, cores * half + kvw)
    weights_old = lax.all_gather(weights_old, "zhi", axis=0, tiled=True)
    mine, weights_old = together(mine, weights_old)

    other = local(
        functools.partial(other_kernel, half),
        [shape((half, kvw), bf16)],
        mine,
        own_gain[half:, None],
    )[0]
    came = swap_cores(other)
    own = local(
        functools.partial(own_kernel, half),
        [shape((half, kvw), f32)],
        mine,
        own_gain[:half, None],
        after=[other],
    )[0]
    partial = local(add_kernel, [shape((half, kvw), bf16)], own, came)[0]
    grad = lax.psum_scatter(partial, "zhi", scatter_dimension=0, tiled=True)
    weights_other = swap_cores(weights_old)

    mixed, sums = local(
        functools.partial(upstream_kernel, half),
        [shape((all_toks, cores * half), f32), shape((group, 8, all_toks), f32)],
        mine,
        weights_old,
        weights_other,
        own_gain[None],
        after=[partial],
    )
    sums = exchange(sums, "x")
    parts = local(
        functools.partial(branch_kernel, (far, rows, width)),
        [shape((layers_y, all_toks, cores * rows), bf16)],
        mine,
        mixed,
        sums,
    )[0]
    next_flat, parts = together(next_acts[:, 0].reshape(toks, width), parts)
    came = exchange(parts, "y")

    fresh_blocks = local(
        functools.partial(fresh_kernel, (far, group, cores, rows)),
        [shape((toks, cores * half), bf16)] * group,
        reward_ids,
        next_flat,
        norm_gain,
        reward_table,
        scratch=[pltpu.VMEM((toks, width), bf16)],
    )
    fresh_normed = shift(fresh_blocks, "x")

    top_shape = shape((all_toks, cores * rows), bf16)
    top = local(top_kernel, [top_shape], came, after=fresh_blocks[:1])[0]
    behind = [from_behind(top, "zlo", 1)]

    first_axes = ("zlo", "zhi")
    last_axes = ("y", "x", "core")
    tile = (8, 128)
    squares = local(
        squares_kernel, [shape((lax.axis_size(first_axes),) + tile, f32)], grad, after=[top] + fresh_normed[1:]
    )[0]
    squares = exchange(squares, first_axes)
    squares = local(relay_kernel, [shape((lax.axis_size(last_axes),) + tile, f32)], squares)[0]
    pair = local(pair_kernel, [top_shape], top, behind[0], after=[squares])[0]
    behind.append(from_behind(pair, "zlo", 2))
    squares = exchange(squares, last_axes)
    suffix = local(
        functools.partial(suffix_kernel, group),
        [shape((layers_y * group, toks, cores * rows), bf16)],
        came,
        *behind,
    )[0]
    shard = shape((rows, kvw), f32)
    moment1_new, moment2_new, weights_new = local(
        functools.partial(adam_kernel, lax.axis_size(section) * width * kvw),
        [shard, shard, shape((rows, kvw), bf16)],
        squares,
        grad,
        master[0],
        moment1[0],
        moment2[0],
        after=[suffix],
    )
    weights_new, suffix = together(weights_new, suffix)
    weights_new = lax.all_gather(weights_new, "zhi", axis=0, tiled=True)
    back = exchange(suffix, ("y", "x"))

    weights_other = swap_cores(weights_new)
    first = local(
        functools.partial(first_kernel, half),
        [shape((group, toks, kvw), f32)],
        *fresh_normed,
        weights_new,
    )[0]
    fresh = local(
        functools.partial(second_kernel, half),
        [shape((group, toks, kvw), bf16)],
        *fresh_normed,
        weights_other,
        first,
    )[0]
    fresh, back = together(fresh, back)
    fresh = jnp.sum(exchange(fresh, "x").astype(f32), axis=0).astype(bf16)
    fresh_values = fresh.reshape(micro, 1, tok_dev, kvw)

    input_grads = local(
        functools.partial(join_kernel, rows), [shape((toks, width), bf16)], back
    )[0].reshape(micro, 1, tok_dev, width)
    return (input_grads, moment1_new[None], moment2_new[None], fresh_values)


def solution(mesh):
    fine = Mesh(mesh.devices.reshape(factors["section"] + factors["dp"]), axes)
    return jax.shard_map(
        per_device,
        mesh=fine,
        in_specs=(
            P(None, section, dp, None),
            P(section, None),
            P(None, section, dp, None),
            P(section, dp, None),
            P(section, dp, None),
            P(section, dp, None),
            P(None, section, dp, None),
            P(),
            P(),
        ),
        out_specs=(
            P(None, section, dp, None),
            P(section, dp, None),
            P(section, dp, None),
            P(None, section, dp, None),
        ),
        check_vma=False,
    )
```

```python
import functools

import jax
import jax.numpy as jnp
from jax import lax
from jax.experimental import pallas as pl
from jax.experimental.pallas import tpu as pltpu
from jax.sharding import Mesh
from jax.sharding import PartitionSpec as P

rms_epsilon = 1e-05
clip_level = 1.0
beta_first = 0.9
beta_second = 0.95
learn_rate = 0.001
decay_rate = 0.01
adam_epsilon = 1e-08
bias_first = 1.0 - 0.9**10
bias_second = 1.0 - 0.95**10

factors = {"section": (4, 4), "dp": (4, 4, 2)}
axes = ("zlo", "y", "zhi", "x", "core")
section = ("zlo", "y")
dp = ("zhi", "x", "core")
near = ("x", "core")
heavy = 2 * 10**10
f32 = jnp.float32
bf16 = jnp.bfloat16


def exchange(blocks, axis):
    return lax.all_to_all(blocks, axis, 0, 0)


def shifts(size):
    return sorted(range(1, size), key=lambda k: -min(k, size - k))


def shift(parts, axis):
    size = len(parts)
    came = [parts[0]] + [None] * (size - 1)
    for k in shifts(size):
        came[k] = lax.ppermute(parts[k], axis, [(i, (i + k) % size) for i in range(size)])
    return came


def swap_cores(block):
    return lax.ppermute(block, "core", [(0, 1), (1, 0)])


def from_behind(block, axis, distance):
    size = lax.axis_size(axis)
    return lax.ppermute(block, axis, [(i + distance, i) for i in range(size - distance)])


def together(*values):
    return lax.optimization_barrier(values)


def inverse_rms(floats):
    return lax.rsqrt(jnp.mean(floats * floats, axis=-1, keepdims=True) + rms_epsilon)


def local(kernel, out_shapes, *arrays, weight=0, scratch=(), after=()):
    def body(*refs):
        kernel(*refs[: len(arrays)], *refs[len(arrays) + len(after) :])

    return pl.pallas_call(
        body,
        out_shape=out_shapes,
        in_specs=[
            pl.BlockSpec(memory_space=pltpu.SMEM if a.dtype == jnp.int32 else pltpu.VMEM)
            for a in arrays
        ]
        + [pl.BlockSpec(memory_space=pl.ANY)] * len(after),
        out_specs=[pl.BlockSpec(memory_space=pltpu.VMEM)] * len(out_shapes),
        scratch_shapes=scratch,
        compiler_params=pltpu.CompilerParams(vmem_limit_bytes=48 * 1024 * 1024),
        cost_estimate=pl.CostEstimate(flops=weight, bytes_accessed=0, transcendentals=0),
    )(*arrays, *after)


def strip_at(start, rows):
    return pl.ds(pl.multiple_of(start, rows), rows)


def split_kernel(sizes, acts, values, master, out, weights):
    far, group, cores, rows = sizes
    core = lax.axis_index("core")
    half = far * rows
    weights[...] = master[...].astype(bf16)
    floats = acts[...].astype(f32)
    scaled = (values[...].astype(f32) * inverse_rms(floats)).astype(bf16)
    for x in range(group):
        for z in range(far):
            for c in range(cores):
                start = ((z * group + x) * cores + ((core + c) & (cores - 1))) * rows
                out[x, :, c * half + z * rows : c * half + (z + 1) * rows] = acts[
                    :, strip_at(start, rows)
                ]
        out[x, :, cores * half :] = scaled


def split(sizes, acts, values, master):
    far, group, cores, rows = sizes
    toks, width = acts.shape
    kvw = values.shape[1]
    steps = 4
    cut = toks // steps
    lanes = cores * far * rows + kvw
    return pl.pallas_call(
        functools.partial(split_kernel, sizes),
        grid=(steps,),
        out_shape=[
            jax.ShapeDtypeStruct((group, toks, lanes), bf16),
            jax.ShapeDtypeStruct((rows, kvw), bf16),
        ],
        in_specs=[
            pl.BlockSpec((cut, width), lambda i: (i, 0)),
            pl.BlockSpec((cut, kvw), lambda i: (i, 0)),
            pl.BlockSpec((rows // steps, kvw), lambda i: (i, 0)),
        ],
        out_specs=[
            pl.BlockSpec((group, cut, lanes), lambda i: (0, i, 0)),
            pl.BlockSpec((rows // steps, kvw), lambda i: (i, 0)),
        ],
        compiler_params=pltpu.CompilerParams(vmem_limit_bytes=63 * 1024 * 1024),
        cost_estimate=pl.CostEstimate(flops=0, bytes_accessed=0, transcendentals=0),
    )(acts, values, master)


def other_kernel(half, mine, gain, out):
    left = mine[:, half : 2 * half]
    part = lax.dot_general(
        left, mine[:, 2 * half :], (((0,), (0,)), ((), ())), preferred_element_type=f32
    )
    out[...] = (part * gain[...]).astype(bf16)


def own_kernel(half, mine, gain, out):
    part = lax.dot_general(
        mine[:, :half], mine[:, 2 * half :], (((0,), (0,)), ((), ())), preferred_element_type=f32
    )
    out[...] = part * gain[...]


def add_kernel(own, came, out):
    out[...] = (own[...] + came[...].astype(f32)).astype(bf16)


def upstream_kernel(half, mine, own, other, gain, mixed, sums):
    values = mine[:, 2 * half :]
    squares, products = 0.0, 0.0
    for c, weights in enumerate((own, other)):
        cols = slice(c * half, (c + 1) * half)
        part = lax.dot_general(
            values, weights[...], (((1,), (1,)), ((), ())), preferred_element_type=f32
        )
        part = part * gain[:, cols]
        mixed[:, cols] = part
        floats = mine[:, cols].astype(f32)
        squares = squares + jnp.sum(floats * floats, axis=1, keepdims=True)
        products = products + jnp.sum(floats * part, axis=1, keepdims=True)
    lane = lax.broadcasted_iota(jnp.int32, (mine.shape[0], 128), 1)
    both = jnp.where(lane == 0, squares, jnp.where(lane == 1, products, 0.0))
    for x in range(sums.shape[0]):
        sums[x] = both.T[:8]


def branch_kernel(sizes, mine, mixed, sums, out):
    far, rows, width = sizes
    half = far * rows
    both = jnp.concatenate([jnp.sum(sums[...], axis=0)] * 16, axis=0).T
    inv = lax.rsqrt(both[:, 0:1] / width + rms_epsilon)
    pull = inv * (inv * (both[:, 1:2] / width))
    for z in range(far):
        for c in range(mixed.shape[1] // half):
            cols = slice(c * half + z * rows, c * half + (z + 1) * rows)
            block = mixed[:, cols] - mine[:, cols].astype(f32) * pull
            out[z, :, c * rows : (c + 1) * rows] = block.astype(bf16)


def fresh_kernel(sizes, ids, acts, gain, table, *refs):
    *outs, normed = refs
    far, group, cores, rows = sizes
    micro = ids.shape[0]
    half = far * rows
    floats = acts[...].astype(f32)
    toks = floats.shape[0]
    row = lax.broadcasted_iota(jnp.int32, (toks, 1), 0)
    for m in range(micro):
        bin_id = ids[m, lax.axis_index(dp)]
        embed = jnp.zeros((1, floats.shape[1]), f32)
        for b in range(table.shape[0]):
            embed = jnp.where(bin_id == b, table[b : b + 1, :].astype(f32), embed)
        first = jnp.logical_and(row == m * (toks // micro), lax.axis_index(section) == 0)
        floats = jnp.where(first, embed, floats)
    normed[...] = (floats * inverse_rms(floats) * gain[...]).astype(bf16)
    for k, out in enumerate(outs):
        x = (lax.axis_index("x") + k) & (group - 1)
        for z in range(far):
            for c in range(cores):
                start = ((z * group + x) * cores + ((lax.axis_index("core") + c) & (cores - 1))) * rows
                out[:, c * half + z * rows : c * half + (z + 1) * rows] = normed[
                    :, strip_at(start, rows)
                ]


def first_kernel(half, *refs):
    *blocks, weights, out = refs
    for k, block in enumerate(blocks):
        part = jnp.dot(block[:, :half], weights[...], preferred_element_type=f32)
        out[(lax.axis_index("x") - k) & (len(blocks) - 1)] = part


def second_kernel(half, *refs):
    *blocks, weights, first, out = refs
    for k, block in enumerate(blocks):
        x = (lax.axis_index("x") - k) & (len(blocks) - 1)
        part = jnp.dot(block[:, half:], weights[...], preferred_element_type=f32)
        out[x] = (first[x] + part).astype(bf16)


def top_kernel(came, out):
    out[...] = jnp.sum(came[...].astype(f32), axis=0).astype(bf16)


def pair_kernel(top, behind, out):
    out[...] = (top[...].astype(f32) + behind[...].astype(f32)).astype(bf16)


def suffix_kernel(group, came, *refs):
    *parts, out = refs
    block = sum(part[...].astype(f32) for part in parts)
    toks = out.shape[1]
    for layer in reversed(range(came.shape[0])):
        block = block + came[layer].astype(f32)
        for x in range(group):
            out[layer * group + x] = block[x * toks : (x + 1) * toks].astype(bf16)


def squares_kernel(grad, out):
    floats = grad[...].astype(f32)
    out[...] = jnp.broadcast_to(jnp.sum(floats * floats), out.shape)


def relay_kernel(sums, out):
    out[...] = jnp.broadcast_to(jnp.sum(sums[...], axis=0, keepdims=True), out.shape)


def adam_kernel(entries, sums, grad, master, first, second, first_new, second_new, weights):
    squares = jnp.sum(sums[...], axis=0)
    clip = jnp.minimum(1.0, clip_level / jnp.sqrt(squares / entries + 1e-12))[0:1, 0:1]
    clipped = grad[...].astype(f32) * clip
    moment1 = beta_first * first[...] + (1.0 - beta_first) * clipped
    moment2 = beta_second * second[...] + (1.0 - beta_second) * clipped * clipped
    first_new[...] = moment1
    second_new[...] = moment2
    update = (
        moment1 / bias_first / (jnp.sqrt(moment2 / bias_second) + adam_epsilon)
        + decay_rate * master[...]
    )
    weights[...] = (master[...] - learn_rate * update).astype(bf16)


def join_kernel(rows, back, out):
    cores = back.shape[2] // rows
    for j in range(back.shape[0]):
        for c in range(cores):
            start = (j * cores + ((lax.axis_index("core") + c) & (cores - 1))) * rows
            out[:, strip_at(start, rows)] = back[j, :, c * rows : (c + 1) * rows]


def per_device(
    acts, norm_gain, value_grads, master, moment1, moment2, next_acts, reward_table, reward_ids
):
    micro, _, tok_dev, width = acts.shape
    kvw = value_grads.shape[3]
    toks = micro * tok_dev
    far = lax.axis_size("zhi")
    group = lax.axis_size("x")
    cores = lax.axis_size("core")
    layers_y = lax.axis_size("y")
    rows = width // (far * group * cores)
    half = far * rows
    all_toks = group * toks
    core, spot_x = lax.axis_index("core"), lax.axis_index("x")
    shape = jax.ShapeDtypeStruct
    gain = norm_gain[0]

    def of_features(block):
        split = block.reshape(block.shape[:-1] + (far, group, cores, rows))
        split = lax.dynamic_index_in_dim(split, spot_x, split.ndim - 3, False)
        halves = [
            lax.dynamic_index_in_dim(split, core ^ c, split.ndim - 2, False) for c in range(cores)
        ]
        return jnp.concatenate([h.reshape(block.shape[:-1] + (half,)) for h in halves], axis=-1)

    own_gain = of_features(gain)

    flat = acts[:, 0].reshape(toks, width)
    blocks, weights_old = split(
        (far, group, cores, rows), flat, value_grads[:, 0].reshape(toks, kvw), master[0]
    )
    mine = exchange(blocks, "x").reshape(all_toks, cores * half + kvw)
    weights_old = lax.all_gather(weights_old, "zhi", axis=0, tiled=True)
    mine, weights_old = together(mine, weights_old)

    other = local(
        functools.partial(other_kernel, half),
        [shape((half, kvw), bf16)],
        mine,
        own_gain[half:, None],
    )[0]
    came = swap_cores(other)
    own = local(
        functools.partial(own_kernel, half),
        [shape((half, kvw), f32)],
        mine,
        own_gain[:half, None],
        after=[other],
    )[0]
    partial = local(add_kernel, [shape((half, kvw), bf16)], own, came)[0]
    grad = lax.psum_scatter(partial, "zhi", scatter_dimension=0, tiled=True)
    weights_other = swap_cores(weights_old)

    mixed, sums = local(
        functools.partial(upstream_kernel, half),
        [shape((all_toks, cores * half), f32), shape((group, 8, all_toks), f32)],
        mine,
        weights_old,
        weights_other,
        own_gain[None],
        after=[partial],
    )
    sums = exchange(sums, "x")
    parts = local(
        functools.partial(branch_kernel, (far, rows, width)),
        [shape((layers_y, all_toks, cores * rows), bf16)],
        mine,
        mixed,
        sums,
    )[0]
    next_flat, parts = together(next_acts[:, 0].reshape(toks, width), parts)
    came = exchange(parts, "y")

    fresh_blocks = local(
        functools.partial(fresh_kernel, (far, group, cores, rows)),
        [shape((toks, cores * half), bf16)] * group,
        reward_ids,
        next_flat,
        norm_gain,
        reward_table,
        scratch=[pltpu.VMEM((toks, width), bf16)],
    )
    fresh_normed = shift(fresh_blocks, "x")

    top_shape = shape((all_toks, cores * rows), bf16)
    top = local(top_kernel, [top_shape], came, after=fresh_blocks[:1])[0]
    behind = [from_behind(top, "zlo", 1)]

    first_axes = ("zlo", "zhi")
    last_axes = ("y", "x", "core")
    tile = (1, 128)
    squares = local(
        squares_kernel, [shape((lax.axis_size(first_axes),) + tile, f32)], grad, after=[top] + fresh_normed[1:]
    )[0]
    squares = exchange(squares, first_axes)
    squares = local(relay_kernel, [shape((lax.axis_size(last_axes),) + tile, f32)], squares)[0]
    pair = local(pair_kernel, [top_shape], top, behind[0], after=[squares])[0]
    behind.append(from_behind(pair, "zlo", 2))
    squares = exchange(squares, last_axes)
    suffix = local(
        functools.partial(suffix_kernel, group),
        [shape((layers_y * group, toks, cores * rows), bf16)],
        came,
        *behind,
    )[0]
    shard = shape((rows, kvw), f32)
    moment1_new, moment2_new, weights_new = local(
        functools.partial(adam_kernel, lax.axis_size(section) * width * kvw),
        [shard, shard, shape((rows, kvw), bf16)],
        squares,
        grad,
        master[0],
        moment1[0],
        moment2[0],
        after=[suffix],
    )
    weights_new, suffix = together(weights_new, suffix)
    weights_new = lax.all_gather(weights_new, "zhi", axis=0, tiled=True)
    back = exchange(suffix, ("y", "x"))

    weights_other = swap_cores(weights_new)
    first = local(
        functools.partial(first_kernel, half),
        [shape((group, toks, kvw), f32)],
        *fresh_normed,
        weights_new,
    )[0]
    fresh = local(
        functools.partial(second_kernel, half),
        [shape((group, toks, kvw), bf16)],
        *fresh_normed,
        weights_other,
        first,
    )[0]
    fresh, back = together(fresh, back)
    fresh = jnp.sum(exchange(fresh, "x").astype(f32), axis=0).astype(bf16)
    fresh_values = fresh.reshape(micro, 1, tok_dev, kvw)

    input_grads = local(
        functools.partial(join_kernel, rows), [shape((toks, width), bf16)], back
    )[0].reshape(micro, 1, tok_dev, width)
    return (input_grads, moment1_new[None], moment2_new[None], fresh_values)


def solution(mesh):
    fine = Mesh(mesh.devices.reshape(factors["section"] + factors["dp"]), axes)
    return jax.shard_map(
        per_device,
        mesh=fine,
        in_specs=(
            P(None, section, dp, None),
            P(section, None),
            P(None, section, dp, None),
            P(section, dp, None),
            P(section, dp, None),
            P(section, dp, None),
            P(None, section, dp, None),
            P(),
            P(),
        ),
        out_specs=(
            P(None, section, dp, None),
            P(section, dp, None),
            P(section, dp, None),
            P(None, section, dp, None),
        ),
        check_vma=False,
    )
```
